32 devices in a mesh: groups: 2 (over y), seq: 4 (over z), rows: 2 (over x), cfg: 2 (over core).
Axes of the slice: x: 2, y: 2, z: 4, core: 2. Of those that a mesh axis runs over, the one named last changes fastest.
Arguments:
- hidden: bfloat16 [2, 4096, 5120], P('cfg', ('groups', 'seq', 'rows')), parts along dimension 1, may hold values from -500 to 500
- token_order: int32 [4096], P(('groups', 'seq', 'rows')), parts along dimension 0, may hold values from 0 to 2047, as said below
- noisy_latent: float32 [16, 8, 2048], P(('groups', 'seq'), ('rows', 'cfg')), parts along dimension 0, may hold values from -6 to 6
- head_weight: bfloat16 [5120, 64], replicated, may hold values from -0.078125 to 0.078125
- head_mod: float32 [2, 5120], replicated, may hold values from -2.5 to 2.5
- guidance: float32 [1], replicated, may hold values from 3 to 7
- timestep_index: int32 [1], replicated, may hold values from 0 to 7
- step_table: int32 [9], replicated, may hold values from 0 to 1000, as said below
- vae_mean: float32 [16], replicated, may hold values from -2.5 to 2.5
- vae_std: float32 [16], replicated, may hold values from 1.1 to 3.3
- conv2_weight: float32 [16, 16], replicated, may hold values from -1.5 to 1.5
- conv2_bias: float32 [16], replicated, may hold values from -2.5 to 2.5
- conv1_weight: bfloat16 [27, 16, 384], replicated, may hold values from -0.3125 to 0.3125
- conv1_bias: float32 [384], replicated, may hold values from -2.5 to 2.5
Outputs:
- decoded: bfloat16 [16, 8, 128, 384], P(('groups', 'seq'), ('rows', 'cfg')), parts along dimension 0
The draws below stay inside these ranges and needn't reach their ends.
There are 2 independent parts, one for each index of `groups`. The reference program is written for one: setup_inputs(seed, part) draws one part's arguments, and reference() takes and returns one part's arrays. A program takes and returns all parts, laid end to end along the dimension named above; an argument that names none is the same for every part. Nothing has to cross between parts.
Inputs may be any that keep to these rules, and one draw needn't show every extreme that they name: `token_order`: a permutation of the 2048 cells, cell f * 4 * 64 + i * 64 + j being token column j of token row i of frame f; positions k * 256 to (k + 1) * 256 - 1 with k = s * 2 + r hold exactly the cells of frames s * 2 to (s + 1) * 2 - 1 and token rows r * 2 to (r + 1) * 2 - 1. `step_table`: strictly decreasing from 1000 to 0; consecutive entries differ by 90 or more.
All inputs are finite; a program needn't handle non-finite values.
Results may differ from the reference program's by a relative error of at most 0.0053.
Values may be sent and summed in bfloat16 or wider, within the bound.
A program may use at most 64 MiB of HBM per device.

```python
import math
import jax
import jax.numpy as jnp
from jax import lax

D = 5120
LAT_C = 16
VAE_CH = 384
PATCH_OUT = 64
FR_DEV = 2
TR_DEV = 2
WT = 64
STEPS = 8
TOK_DEV = 256
FR = 8
HT = 4
TOKENS = 2048
LH = 8
LW = 128


def draw_hidden(key, part):
    key_base, key_rows, key_cols = jax.random.split(key, 3)
    full_shape = (2, TOKENS, D)
    row_scale = jnp.exp(jax.random.uniform(key_rows, (2, TOKENS, 1), jnp.float32) * math.log(10.0))
    col_scale = jnp.exp(jax.random.uniform(key_cols, (1, 1, D), jnp.float32) * math.log(10.0))
    base_values = jnp.clip(jax.random.normal(key_base, full_shape, jnp.float32), -5.0, 5.0)
    return (base_values * row_scale * col_scale).astype(jnp.bfloat16)


def draw_token_order(key, part):
    block_count = TOKENS // TOK_DEV
    block_keys = jax.random.split(jax.random.fold_in(key, 17), block_count)
    orders = jax.vmap(lambda block_key: jax.random.permutation(block_key, TOK_DEV))(block_keys)
    per_frame = HT // TR_DEV
    block_ids = jnp.arange(block_count, dtype=jnp.int32)[:, None]
    seq_block = block_ids // per_frame
    row_block = block_ids % per_frame
    frame_local = orders // (TR_DEV * WT)
    row_local = orders // WT % TR_DEV
    col_local = orders % WT
    cell_ids = (seq_block * FR_DEV + frame_local) * HT * WT + (row_block * TR_DEV + row_local) * WT + col_local
    return cell_ids.reshape(TOKENS).astype(jnp.int32)


def draw_step_table(key, part):
    step_gaps = jax.random.randint(jax.random.fold_in(key, 29), (STEPS - 1,), 90, 131)
    positions = 1000 - jnp.concatenate([jnp.zeros((1,), jnp.int32), jnp.cumsum(step_gaps).astype(jnp.int32)])
    return jnp.concatenate([positions, jnp.zeros((1,), jnp.int32)]).astype(jnp.int32)


def shard_levels(key, dims, cuts, smallest, top_value):
    factor_of, own = 1.0, jax.random.fold_in(key, 6)
    for position, parts in cuts:
        steps = jnp.exp(jax.random.uniform(jax.random.fold_in(own, position), (parts,), jnp.float32, smallest / len(cuts), top_value / len(cuts)))
        factor_of = factor_of * jnp.repeat(steps, dims[position] // parts).reshape([-1 if axis == position else 1 for axis in range(len(dims))])
    return factor_of


def gaussian(key, dims, scale, reach, shards=(), kind=jnp.bfloat16):
    drawn = jax.random.normal(key, dims, jnp.float32) * scale
    if len(shards) > 0:
        drawn = shard_levels(key, dims, shards, -0.22, 0.18) * drawn
    return jnp.clip(drawn, min=-reach, max=reach).astype(kind)


def setup_inputs(seed: int = 0, part: int = 0) -> dict:
    key_of = jax.random.split(jax.random.key(seed), 15)
    part_splits = jax.random.split(jax.random.fold_in(key_of[14], part), 15)
    return {
        "hidden": draw_hidden(jax.random.fold_in(jax.random.fold_in(key_of[14], part), 71), part),
        "token_order": draw_token_order(jax.random.fold_in(jax.random.fold_in(key_of[14], part), 71), part),
        "noisy_latent": gaussian(part_splits[2], (FR, LH, LW * LAT_C), 1.0, 6.0, ((0, 4), (1, 4)), jnp.float32),
        "head_weight": gaussian(key_of[3], (D, PATCH_OUT), D ** -0.5, 0.078125),
        "head_mod": gaussian(key_of[4], (2, D), 0.5, 2.5, (), jnp.float32),
        "guidance": jnp.clip(jax.random.uniform(key_of[5], (1,), jnp.float32, 3.0, 7.0), 3.0, 7.0),
        "timestep_index": jax.random.randint(key_of[6], (1,), 0, STEPS).astype(jnp.int32),
        "step_table": draw_step_table(jax.random.fold_in(key_of[14], 71), part),
        "vae_mean": gaussian(key_of[8], (LAT_C,), 0.5, 2.5, (), jnp.float32),
        "vae_std": jnp.clip(jnp.exp(jax.random.uniform(key_of[9], (LAT_C,), jnp.float32, math.log(1.1), math.log(3.3))), 1.1, 3.3),
        "conv2_weight": gaussian(key_of[10], (LAT_C, LAT_C), LAT_C ** -0.5, 1.5, (), jnp.float32),
        "conv2_bias": gaussian(key_of[11], (LAT_C,), 0.5, 2.5, (), jnp.float32),
        "conv1_weight": gaussian(key_of[12], (27, LAT_C, VAE_CH), (27 * LAT_C) ** -0.5, 0.3125),
        "conv1_bias": gaussian(key_of[13], (VAE_CH,), 0.5, 2.5, (), jnp.float32),
    }


def head_rows(row_block, head_weight, head_mod):
    values = row_block.astype(jnp.float32)
    center = lax.optimization_barrier(jnp.mean(values, axis=-1, keepdims=True))
    spread = lax.optimization_barrier(jnp.mean(jnp.square(values - center), axis=-1, keepdims=True))
    normed = (values - center) * lax.rsqrt(spread + 1e-06)
    head_in = (normed * (1.0 + head_mod[1]) + head_mod[0]).astype(jnp.bfloat16)
    return jnp.dot(head_in, head_weight, preferred_element_type=jnp.float32)

def conv_taps(padded, frames, row_count, col_count):
    pieces = []
    for step_time in range(3):
        for step_row in range(3):
            for step_col in range(3):
                pieces.append(padded[step_time:step_time + frames, step_row:step_row + row_count, step_col:step_col + col_count, :])
    return jnp.concatenate(pieces, axis=-1)

def reference(hidden, token_order, noisy_latent, head_weight, head_mod, guidance, timestep_index, step_table, vae_mean, vae_std, conv2_weight, conv2_bias, conv1_weight, conv1_bias):

    def one_block(block_index):
        row_block = lax.dynamic_slice_in_dim(hidden, block_index * TOK_DEV, TOK_DEV, 1)
        result = head_rows(row_block.reshape(2 * TOK_DEV, D), head_weight, head_mod).reshape(2, TOK_DEV, PATCH_OUT)
        return result[1] + guidance[0] * (result[0] - result[1])
    velocity = lax.map(one_block, jnp.arange(TOKENS // TOK_DEV, dtype=jnp.int32)).reshape(TOKENS, PATCH_OUT)
    cell_values = jnp.zeros((TOKENS, PATCH_OUT), jnp.float32).at[token_order].set(velocity)
    latent_velocity = cell_values.reshape(FR, HT, WT, 2, 2, LAT_C).transpose(0, 1, 3, 2, 4, 5).reshape(FR, LH, LW * LAT_C)
    step_index = timestep_index[0]
    sigma_now = step_table[step_index].astype(jnp.float32) / 1000.0
    sigma_next = step_table[step_index + 1].astype(jnp.float32) / 1000.0
    stepped = noisy_latent + (sigma_next - sigma_now) * latent_velocity
    channels = stepped.reshape(FR, LH, LW, LAT_C) * vae_std + vae_mean
    mixed_lat = jnp.einsum('fyxc,cd->fyxd', channels, conv2_weight, precision=lax.Precision.HIGHEST) + conv2_bias
    latent_in = mixed_lat.astype(jnp.bfloat16)
    padded = jnp.pad(latent_in, ((2, 0), (1, 1), (1, 1), (0, 0)))
    kernel = conv1_weight.reshape(27 * LAT_C, VAE_CH)

    def one_frame(frame_index):
        window = lax.dynamic_slice_in_dim(padded, frame_index, 3, 0)
        tap_columns = conv_taps(window, 1, LH, LW).reshape(LH * LW, 27 * LAT_C)
        result = jnp.dot(tap_columns, kernel, preferred_element_type=jnp.float32) + conv1_bias
        return result.astype(jnp.bfloat16).reshape(LH, LW, VAE_CH)
    return lax.map(one_frame, jnp.arange(FR, dtype=jnp.int32))
```

```python
import functools

import jax
import jax.numpy as jnp
from jax import lax
from jax.experimental import pallas as pl
from jax.experimental.pallas import tpu as pltpu
from jax.sharding import PartitionSpec as P

F32 = jnp.float32
BF16 = jnp.bfloat16
LANES = 128
EXTRA = 16


def split_bf16(value):
    high = value.astype(BF16)
    low = (value - high.astype(F32)).astype(BF16)
    return high, low


def dot_nt(left, right):
    return lax.dot_general(left, right, (((1,), (1,)), ((), ())), preferred_element_type=F32)


def dot_nn(left, right):
    return jnp.dot(left, right, preferred_element_type=F32)


def kernel(
    sizes,
    hidden_hbm,
    order_hbm,
    noisy_hbm,
    weight_hbm,
    mod_hbm,
    guidance_hbm,
    index_hbm,
    table_hbm,
    mean_hbm,
    std_hbm,
    mix_hbm,
    mix_bias_hbm,
    conv_hbm,
    conv_bias_hbm,
    out_ref,
    x_buf,
    w_buf,
    rhs_buf,
    order_buf,
    noisy_buf,
    mod_buf,
    guidance_buf,
    index_buf,
    table_buf,
    mean_buf,
    std_buf,
    mix_buf,
    mix_bias_buf,
    conv_buf,
    conv_bias_buf,
    latent_buf,
    taps_buf,
    cells_buf,
    partner_buf,
    edge_buf,
    halo_buf,
    wide_buf,
    local_sem,
    chunk_sem,
    send_sem,
    recv_sem,
):
    seq_count, row_count, cfg_count, token_rows, token_cols, frames, chunks = sizes
    tokens = hidden_hbm.shape[1]
    width = hidden_hbm.shape[2]
    patch = weight_hbm.shape[0]
    chan = mix_hbm.shape[0]
    out_chan = conv_hbm.shape[2]
    slab_count = row_count * cfg_count
    step = width // chunks

    seq = lax.axis_index("seq")
    row = lax.axis_index("rows")
    half = lax.axis_index("cfg")
    slab = row * cfg_count + half

    small = []
    for source, target in (
        (mod_hbm, mod_buf),
        (order_hbm, order_buf),
        (noisy_hbm, noisy_buf),
        (guidance_hbm, guidance_buf),
        (index_hbm, index_buf),
        (table_hbm, table_buf),
        (mean_hbm, mean_buf),
        (std_hbm, std_buf),
        (mix_hbm, mix_buf),
        (mix_bias_hbm, mix_bias_buf),
        (conv_bias_hbm, conv_bias_buf),
        (conv_hbm, conv_buf),
    ):
        small.append(pltpu.make_async_copy(source, target, local_sem.at[len(small)]))
    loads = []
    for part in range(chunks):
        columns = pl.ds(part * step, step)
        loads.append(
            (
                pltpu.make_async_copy(
                    weight_hbm.at[:, columns], w_buf.at[:, columns], chunk_sem.at[0, part]
                ),
                pltpu.make_async_copy(
                    hidden_hbm.at[0, :, columns],
                    x_buf.at[pl.ds(0, tokens), columns],
                    chunk_sem.at[1, part],
                ),
            )
        )
    small[0].start()
    for weight_copy, hidden_copy in loads:
        weight_copy.start()
        hidden_copy.start()
    for copy in small[1:]:
        copy.start()

    barrier = pltpu.get_barrier_semaphore()

    def present(seq_step, slab_step):
        ok = jnp.bool_(True)
        if seq_step:
            ok = jnp.logical_and(ok, seq > 0 if seq_step < 0 else seq < seq_count - 1)
        if slab_step:
            ok = jnp.logical_and(ok, slab > 0 if slab_step < 0 else slab < slab_count - 1)
        return ok

    def place(seq_step, slab_step):
        other = slab + slab_step + cfg_count
        return {
            "seq": seq + seq_step,
            "rows": lax.div(other, cfg_count) - 1,
            "cfg": lax.rem(other, cfg_count),
        }

    around = [(a, b) for a in (-1, 0, 1) for b in (-1, 0, 1) if a or b]
    for offset in around:

        @pl.when(present(*offset))
        def _(offset=offset):
            pl.semaphore_signal(
                barrier, inc=1, device_id=place(*offset), device_id_type=pl.DeviceIdType.MESH
            )

    sends = ((0, 1), (0, -1), (1, 0), (1, 1), (1, -1))
    for slot, (seq_step, slab_step) in enumerate(sends):

        @pl.when(jnp.logical_not(present(-seq_step, -slab_step)))
        def _(slot=slot):
            halo_buf[slot] = jnp.zeros(halo_buf.shape[1:], BF16)

    small[0].wait()
    scale = 1.0 + mod_buf[1:2, :]
    shift_high, shift_low = split_bf16(mod_buf[0:1, :])
    pick = lax.broadcasted_iota(jnp.int32, (EXTRA, width), 0)
    x_buf[tokens : tokens + EXTRA, :] = jnp.where(
        pick == 0,
        shift_high.astype(F32),
        jnp.where(pick == 1, shift_low.astype(F32), jnp.where(pick == 2, 1.0, 0.0)),
    ).astype(BF16)
    ones_row = lax.broadcasted_iota(jnp.int32, (EXTRA, width), 0) == 0
    rhs_buf[2 * patch : 2 * patch + EXTRA, :] = jnp.where(ones_row, 1.0, 0.0).astype(BF16)

    block = 64
    blocks = tokens // block
    product = jnp.zeros((tokens + EXTRA, rhs_buf.shape[0]), F32)
    centers = [None] * blocks
    squares = [jnp.zeros((block, LANES), F32)] * blocks
    for part, (weight_copy, hidden_copy) in enumerate(loads):
        low = part * step
        weight_copy.wait()
        raw = w_buf[:, low : low + step]
        rhs_buf[0:patch, low : low + step] = (
            raw.astype(F32) * scale[:, low : low + step]
        ).astype(BF16)
        rhs_buf[patch : 2 * patch, low : low + step] = raw
        hidden_copy.wait()
        product = product + dot_nt(x_buf[:, low : low + step], rhs_buf[:, low : low + step])
        for index in range(blocks):
            rows = slice(index * block, (index + 1) * block)
            if part == 0:
                total = jnp.zeros((block, LANES), F32)
                for lane in range(0, step, LANES):
                    total = total + x_buf[rows, lane : lane + LANES].astype(F32)
                center = jnp.sum(total, axis=1, keepdims=True) * (1.0 / step)
                centers[index] = jnp.broadcast_to(center, (block, LANES))
            square = squares[index]
            for lane in range(low, low + step, LANES):
                gap = x_buf[rows, lane : lane + LANES].astype(F32) - centers[index]
                square = square + gap * gap
            squares[index] = square

    center = jnp.concatenate([value[:, 0:1] for value in centers], axis=0)
    spread = jnp.concatenate([jnp.sum(value, axis=1, keepdims=True) for value in squares], axis=0)
    average = product[0:tokens, 2 * patch : 2 * patch + 1] * (1.0 / width)
    spread = spread * (1.0 / width) - jnp.square(average - center)
    inverse = lax.rsqrt(spread + 1e-06)
    column_sum = product[tokens + 2 : tokens + 3, 0:patch]
    both = product[tokens : tokens + 1, :] + product[tokens + 1 : tokens + 2, :]
    offset_row = both[:, patch : 2 * patch]
    head = (product[0:tokens, 0:patch] - average * column_sum) * inverse + offset_row

    for copy in small[1:]:
        copy.wait()
    cell = order_buf[...].astype(F32) + 0.5
    per_frame = float(row_count * token_rows * token_cols)
    frame_all = jnp.floor(cell * (1.0 / per_frame))
    in_frame = cell - frame_all * per_frame
    frame_pos = frame_all - frames * jnp.floor((frame_all + 0.5) * (1.0 / frames))
    row_all = jnp.floor(in_frame * (1.0 / token_cols))
    column = in_frame - 0.5 - row_all * token_cols
    row_pos = row_all - token_rows * jnp.floor((row_all + 0.5) * (1.0 / token_rows))
    target = (frame_pos * token_rows + row_pos) * token_cols + column
    wanted = lax.broadcasted_iota(jnp.int32, (tokens, tokens), 0).astype(F32)
    one_hot = jnp.where(jnp.abs(wanted - target) < 0.25, 1.0, 0.0).astype(BF16)
    head_high, head_low = split_bf16(head)
    placed = dot_nn(one_hot, head_high) + dot_nn(one_hot, head_low)
    per = token_rows * token_cols
    for index in range(token_rows):
        pieces = [
            placed[f * per + index * token_cols : f * per + (index + 1) * token_cols, :]
            for f in range(frames)
        ]
        cells_buf[index] = jnp.concatenate(pieces, axis=1)

    slab_peers = (slab > 0).astype(jnp.int32) + (slab < slab_count - 1).astype(jnp.int32)
    seq_peers = (seq > 0).astype(jnp.int32) + (seq < seq_count - 1).astype(jnp.int32)
    pl.semaphore_wait(barrier, (1 + slab_peers) * (1 + seq_peers) - 1)

    pair = pltpu.make_async_remote_copy(
        src_ref=cells_buf.at[1 - half],
        dst_ref=partner_buf,
        send_sem=send_sem.at[0],
        recv_sem=recv_sem.at[0],
        device_id={"cfg": 1 - half},
        device_id_type=pl.DeviceIdType.MESH,
    )
    pair.start()

    lane = lax.broadcasted_iota(jnp.int32, (noisy_buf.shape[2], LANES), 1)
    span = 2 * chan
    per_line = LANES // span
    groups = noisy_buf.shape[2]
    for jj in range(per_line):
        line = jnp.zeros((groups, LANES), F32)
        for f in range(frames):
            for a in range(2):
                slot = f * 2 + a
                moved = noisy_buf[f, a]
                if (slot - jj) % per_line:
                    moved = pltpu.roll(moved, ((slot - jj) * span) % LANES, 1)
                line = jnp.where((lane >= slot * span) & (lane < (slot + 1) * span), moved, line)
        latent_buf[pl.ds(jj, groups, stride=per_line), :] = line

    repeat = LANES // chan

    def lanes_of(ref):
        return jnp.concatenate([ref[...]] * repeat, axis=1)

    mean_row = lanes_of(mean_buf)
    std_row = lanes_of(std_buf)
    mix_row = lanes_of(mix_bias_buf)
    mix = jnp.concatenate([lanes_of(mix_buf)] * repeat, axis=0)
    mix_in = lax.broadcasted_iota(jnp.int32, (LANES, LANES), 0)
    mix_out = lax.broadcasted_iota(jnp.int32, (LANES, LANES), 1)
    same = lax.div(mix_in, chan) == lax.div(mix_out, chan)
    mix_high, mix_low = split_bf16(jnp.where(same, mix, 0.0))
    mix_both = jnp.concatenate([mix_high, mix_low], axis=1)

    spot = lax.broadcasted_iota(jnp.int32, table_buf.shape, 1)
    table = table_buf[...].astype(F32)
    now = jnp.sum(jnp.where(spot == index_buf[...], table, 0.0), axis=1, keepdims=True)
    later = jnp.sum(jnp.where(spot == index_buf[...] + 1, table, 0.0), axis=1, keepdims=True)
    step_size = later / 1000.0 - now / 1000.0

    position = 0
    for t in range(3):
        for shifted in range(2):
            for u in range(4):
                for e_in in range(2):
                    dx = (2 - 3 * e_in) if shifted else e_in
                    for e_out in range(2):
                        w = dx - e_out + 1
                        columns = slice(e_out * out_chan, (e_out + 1) * out_chan)
                        if u < 3 and 0 <= w <= 2:
                            value = conv_buf[(t * 3 + u) * 3 + w]
                        else:
                            value = jnp.zeros((chan, out_chan), BF16)
                        taps_buf[position : position + chan, columns] = value
                    position += chan

    pair.wait_recv()
    own = cells_buf[half]
    partner = partner_buf[...]
    cond = jnp.where(half == 0, own, partner)
    free = jnp.where(half == 0, partner, own)
    velocity = free + guidance_buf[...] * (cond - free)
    stepped = latent_buf[...] + step_size * velocity
    channels = stepped * std_row + mean_row
    high, low = split_bf16(channels)
    mixed = dot_nn(jnp.concatenate([high, low], axis=0), mix_both)
    mixed = mixed[0:token_cols, 0:LANES] + (
        mixed[0:token_cols, LANES:] + mixed[token_cols:, 0:LANES]
    )
    latent = (mixed + mix_row).astype(BF16)
    edge_buf[...] = latent

    copies = []
    for slot, (seq_step, slab_step) in enumerate(sends):
        copy = pltpu.make_async_remote_copy(
            src_ref=edge_buf,
            dst_ref=halo_buf.at[slot],
            send_sem=send_sem.at[1 + slot],
            recv_sem=recv_sem.at[1 + slot],
            device_id=place(seq_step, slab_step),
            device_id_type=pl.DeviceIdType.MESH,
        )
        copies.append(copy)
    for slot in (3, 4, 2, 0, 1):
        pl.when(present(*sends[slot]))(copies[slot].start)

    for slot, (seq_step, slab_step) in enumerate(sends):
        pl.when(present(-seq_step, -slab_step))(copies[slot].wait_recv)

    lane = lax.broadcasted_iota(jnp.int32, (token_cols, LANES), 1)
    line = lax.broadcasted_iota(jnp.int32, (token_cols, LANES), 0)
    odd = lax.rem(lax.div(lane, chan), 2) == 1

    def turned(value, amount):
        return pltpu.roll(value, amount % LANES, 1) if amount % LANES else value

    columns_of = []
    for center_block, above, below in (
        (halo_buf[2].astype(F32), halo_buf[3].astype(F32), halo_buf[4].astype(F32)),
        (latent.astype(F32), halo_buf[0].astype(F32), halo_buf[1].astype(F32)),
    ):
        for f in range(frames):
            base = f * 2 * span
            full = turned(center_block, span - base)
            full = jnp.where(lane < span, turned(above, -base - span), full)
            full = jnp.where(lane >= 3 * span, turned(below, 3 * span - base), full)
            before = jnp.where(line == 0, 0.0, pltpu.roll(full, 1, 0))
            after = jnp.where(line == token_cols - 1, 0.0, pltpu.roll(full, token_cols - 1, 0))
            beside = jnp.where(odd, before, after)
            lower = (turned(full, -span), turned(beside, -span))
            columns_of.append(
                (
                    (full.astype(BF16), beside.astype(BF16)),
                    (lower[0].astype(BF16), lower[1].astype(BF16)),
                )
            )
    taps = taps_buf[...]
    bias = conv_bias_buf[...]
    columns = jnp.concatenate(
        [
            jnp.concatenate(
                [piece for t in range(3) for piece in columns_of[f + t][y]], axis=1
            )
            for f in range(frames)
            for y in range(2)
        ],
        axis=0,
    )
    result = dot_nn(columns, taps)
    for f in range(frames):
        for y in range(2):
            first = (f * 2 + y) * token_cols
            for part in range(out_chan // LANES):
                lanes = slice(part * LANES, (part + 1) * LANES)
                for e in range(2):
                    from_lane = e * out_chan + part * LANES
                    wide_buf[part, pl.ds(2 * first + e, token_cols, stride=2), :] = (
                        result[first : first + token_cols, from_lane : from_lane + LANES]
                        + bias[:, lanes]
                    )
                out_ref[f, y, :, lanes] = wide_buf[
                    part, 2 * first : 2 * first + 2 * token_cols, :
                ].astype(BF16)

    pair.wait_send()
    for slot in range(len(sends)):
        pl.when(present(*sends[slot]))(copies[slot].wait_send)


def per_device(
    counts,
    hidden,
    token_order,
    noisy_latent,
    head_weight,
    head_mod,
    guidance,
    timestep_index,
    step_table,
    vae_mean,
    vae_std,
    conv2_weight,
    conv2_bias,
    conv1_weight,
    conv1_bias,
):
    frames, lat_rows, lat_width = noisy_latent.shape
    chan = vae_mean.shape[0]
    tokens, width = hidden.shape[1:]
    patch = head_weight.shape[1]
    out_chan = conv1_weight.shape[2]
    token_cols = lat_width // (2 * chan)
    token_rows = lat_rows * counts[2] // 2
    chunks = 5
    operands = (
        hidden,
        token_order.reshape(1, -1),
        noisy_latent.reshape(frames, lat_rows, lat_width // LANES, LANES),
        head_weight.T,
        head_mod,
        guidance.reshape(1, 1),
        timestep_index.reshape(1, 1),
        step_table.reshape(1, -1),
        vae_mean.reshape(1, -1),
        vae_std.reshape(1, -1),
        conv2_weight,
        conv2_bias.reshape(1, -1),
        conv1_weight,
        conv1_bias.reshape(1, -1),
    )
    block = (token_cols, LANES)
    scratch = [
        pltpu.VMEM((tokens + EXTRA, width), BF16),
        pltpu.VMEM((patch, width), BF16),
        pltpu.VMEM((2 * patch + EXTRA, width), BF16),
        pltpu.VMEM(operands[1].shape, jnp.int32),
        pltpu.VMEM(operands[2].shape, F32),
    ]
    scratch += [pltpu.VMEM(value.shape, value.dtype) for value in operands[4:]]
    scratch += [
        pltpu.VMEM(block, F32),
        pltpu.VMEM((3 * 16 * chan, 2 * out_chan), BF16),
        pltpu.VMEM((token_rows,) + block, F32),
        pltpu.VMEM(block, F32),
        pltpu.VMEM(block, BF16),
        pltpu.VMEM((5,) + block, BF16),
        pltpu.VMEM((out_chan // LANES, frames * lat_rows * 2 * token_cols, LANES), F32),
        pltpu.SemaphoreType.DMA((12,)),
        pltpu.SemaphoreType.DMA((2, chunks)),
        pltpu.SemaphoreType.DMA((6,)),
        pltpu.SemaphoreType.DMA((6,)),
    ]
    sizes = tuple(counts) + (token_rows, token_cols, frames, chunks)
    return pl.pallas_call(
        functools.partial(kernel, sizes),
        out_shape=jax.ShapeDtypeStruct((frames, lat_rows, 2 * token_cols, out_chan), BF16),
        in_specs=[pl.BlockSpec(memory_space=pl.ANY)] * len(operands),
        out_specs=pl.BlockSpec(memory_space=pltpu.VMEM),
        scratch_shapes=scratch,
        compiler_params=pltpu.CompilerParams(
            collective_id=0, has_side_effects=True, vmem_limit_bytes=60 * 1024 * 1024
        ),
        name="guided_step",
    )(*operands)


def solution(mesh):
    counts = (mesh.shape["seq"], mesh.shape["rows"], mesh.shape["cfg"])
    return jax.shard_map(
        functools.partial(per_device, counts),
        mesh=mesh,
        in_specs=(
            P("cfg", ("groups", "seq", "rows"), None),
            P(("groups", "seq", "rows")),
            P(("groups", "seq"), ("rows", "cfg"), None),
            P(),
            P(),
            P(),
            P(),
            P(),
            P(),
            P(),
            P(),
            P(),
            P(),
            P(),
        ),
        out_specs=P(("groups", "seq"), ("rows", "cfg"), None, None),
        check_vma=False,
    )
```

```python
import functools

import jax
import jax.numpy as jnp
from jax import lax
from jax.experimental import pallas as pl
from jax.experimental.pallas import tpu as pltpu
from jax.sharding import PartitionSpec as P

F32 = jnp.float32
BF16 = jnp.bfloat16
LANES = 128
EXTRA = 16


def split_bf16(value):
    high = value.astype(BF16)
    low = (value - high.astype(F32)).astype(BF16)
    return high, low


def dot_nt(left, right):
    return lax.dot_general(left, right, (((1,), (1,)), ((), ())), preferred_element_type=F32)


def dot_nn(left, right):
    return jnp.dot(left, right, preferred_element_type=F32)


def kernel(
    sizes,
    hidden_hbm,
    order_hbm,
    noisy_hbm,
    weight_hbm,
    mod_hbm,
    guidance_ref,
    index_ref,
    table_ref,
    mean_hbm,
    std_hbm,
    mix_hbm,
    mix_bias_hbm,
    conv_hbm,
    conv_bias_hbm,
    out_ref,
    x_buf,
    w_buf,
    rhs_buf,
    order_buf,
    noisy_buf,
    mod_buf,
    mean_buf,
    std_buf,
    mix_buf,
    mix_bias_buf,
    conv_buf,
    conv_bias_buf,
    lines_buf,
    latent_buf,
    taps_buf,
    cells_buf,
    partner_buf,
    edge_buf,
    halo_buf,
    wide_buf,
    local_sem,
    chunk_sem,
    send_sem,
    recv_sem,
):
    seq_count, row_count, cfg_count, token_rows, token_cols, frames, chunks = sizes
    tokens = hidden_hbm.shape[1]
    width = hidden_hbm.shape[2]
    patch = weight_hbm.shape[0]
    chan = mix_hbm.shape[0]
    out_chan = conv_hbm.shape[2]
    slab_count = row_count * cfg_count
    step = width // chunks

    seq = lax.axis_index("seq")
    row = lax.axis_index("rows")
    half = lax.axis_index("cfg")
    slab = row * cfg_count + half

    small = []
    for source, target in (
        (mod_hbm, mod_buf),
        (order_hbm, order_buf),
        (noisy_hbm, noisy_buf),
        (mean_hbm, mean_buf),
        (std_hbm, std_buf),
        (mix_hbm, mix_buf),
        (mix_bias_hbm, mix_bias_buf),
        (conv_bias_hbm, conv_bias_buf),
        (conv_hbm, conv_buf),
    ):
        small.append(pltpu.make_async_copy(source, target, local_sem.at[len(small)]))
    loads = []
    for part in range(chunks):
        columns = pl.ds(part * step, step)
        loads.append(
            (
                pltpu.make_async_copy(
                    weight_hbm.at[:, columns], w_buf.at[:, columns], chunk_sem.at[0, part]
                ),
                pltpu.make_async_copy(
                    hidden_hbm.at[0, :, columns],
                    x_buf.at[pl.ds(0, tokens), columns],
                    chunk_sem.at[1, part],
                ),
            )
        )
    small[0].start()
    for index, (weight_copy, hidden_copy) in enumerate(loads):
        weight_copy.start()
        hidden_copy.start()
        if index == 0:
            for copy in small[1:-1]:
                copy.start()
    small[-1].start()

    barrier = pltpu.get_barrier_semaphore()

    def present(seq_step, slab_step):
        ok = jnp.bool_(True)
        if seq_step:
            ok = jnp.logical_and(ok, seq > 0 if seq_step < 0 else seq < seq_count - 1)
        if slab_step:
            ok = jnp.logical_and(ok, slab > 0 if slab_step < 0 else slab < slab_count - 1)
        return ok

    def place(seq_step, slab_step):
        other = slab + slab_step + cfg_count
        return {
            "seq": seq + seq_step,
            "rows": lax.div(other, cfg_count) - 1,
            "cfg": lax.rem(other, cfg_count),
        }

    around = [(a, b) for a in (-1, 0, 1) for b in (-1, 0, 1) if a or b]
    for offset in around:

        @pl.when(present(*offset))
        def _(offset=offset):
            pl.semaphore_signal(
                barrier, inc=1, device_id=place(*offset), device_id_type=pl.DeviceIdType.MESH
            )

    sends = ((0, 1), (0, -1), (1, 0), (1, 1), (1, -1))
    for slot, (seq_step, slab_step) in enumerate(sends):

        @pl.when(jnp.logical_not(present(-seq_step, -slab_step)))
        def _(slot=slot):
            halo_buf[slot] = jnp.zeros(halo_buf.shape[1:], BF16)

    small[0].wait()
    scale = 1.0 + mod_buf[1:2, :]
    shift_high, shift_low = split_bf16(mod_buf[0:1, :])
    pick = lax.broadcasted_iota(jnp.int32, (EXTRA, width), 0)
    x_buf[tokens : tokens + EXTRA, :] = jnp.where(
        pick == 0,
        shift_high.astype(F32),
        jnp.where(pick == 1, shift_low.astype(F32), jnp.where(pick == 2, 1.0, 0.0)),
    ).astype(BF16)
    ones_row = lax.broadcasted_iota(jnp.int32, (EXTRA, width), 0) == 0
    rhs_buf[2 * patch : 2 * patch + EXTRA, :] = jnp.where(ones_row, 1.0, 0.0).astype(BF16)

    for copy in small[1:-1]:
        copy.wait()
    cell = order_buf[...].astype(F32) + 0.5
    per_frame = float(row_count * token_rows * token_cols)
    frame_all = jnp.floor(cell * (1.0 / per_frame))
    in_frame = cell - frame_all * per_frame
    frame_pos = frame_all - frames * jnp.floor((frame_all + 0.5) * (1.0 / frames))
    row_all = jnp.floor(in_frame * (1.0 / token_cols))
    column = in_frame - 0.5 - row_all * token_cols
    row_pos = row_all - token_rows * jnp.floor((row_all + 0.5) * (1.0 / token_rows))
    target = (frame_pos * token_rows + row_pos) * token_cols + column
    wanted = lax.broadcasted_iota(jnp.int32, (tokens, tokens), 0).astype(F32)
    one_hot = jnp.where(jnp.abs(wanted - target) < 0.25, 1.0, 0.0).astype(BF16)
    for f in range(frames):
        for a in range(2):
            for g in range(lines_buf.shape[2]):
                lines_buf[f, a, g : g + 1, :] = noisy_buf[f, a : a + 1, g * LANES : (g + 1) * LANES]
    lane = lax.broadcasted_iota(jnp.int32, (lines_buf.shape[2], LANES), 1)
    span = 2 * chan
    per_line = LANES // span
    groups = lines_buf.shape[2]
    for jj in range(per_line):
        line = jnp.zeros((groups, LANES), F32)
        for f in range(frames):
            for a in range(2):
                slot = f * 2 + a
                moved = lines_buf[f, a]
                if (slot - jj) % per_line:
                    moved = pltpu.roll(moved, ((slot - jj) * span) % LANES, 1)
                line = jnp.where((lane >= slot * span) & (lane < (slot + 1) * span), moved, line)
        latent_buf[pl.ds(jj, groups, stride=per_line), :] = line

    repeat = LANES // chan

    def lanes_of(ref):
        return jnp.concatenate([ref[...]] * repeat, axis=1)

    mean_row = lanes_of(mean_buf)
    std_row = lanes_of(std_buf)
    mix_row = lanes_of(mix_bias_buf)
    mix = jnp.concatenate([lanes_of(mix_buf)] * repeat, axis=0)
    mix_in = lax.broadcasted_iota(jnp.int32, (LANES, LANES), 0)
    mix_out = lax.broadcasted_iota(jnp.int32, (LANES, LANES), 1)
    same = lax.div(mix_in, chan) == lax.div(mix_out, chan)
    mix_high, mix_low = split_bf16(jnp.where(same, mix, 0.0))
    mix_both = jnp.concatenate([mix_high, mix_low], axis=1)

    at = index_ref[0]
    now = jnp.full((1, LANES), table_ref[at].astype(F32))
    later = jnp.full((1, LANES), table_ref[at + 1].astype(F32))
    step_size = later / 1000.0 - now / 1000.0

    block = 64
    blocks = tokens // block
    product = jnp.zeros((tokens + EXTRA, rhs_buf.shape[0]), F32)
    centers = [None] * blocks
    squares = [jnp.zeros((block, LANES), F32)] * blocks
    for part, (weight_copy, hidden_copy) in enumerate(loads):
        low = part * step
        weight_copy.wait()
        raw = w_buf[:, low : low + step]
        rhs_buf[0:patch, low : low + step] = (
            raw.astype(F32) * scale[:, low : low + step]
        ).astype(BF16)
        rhs_buf[patch : 2 * patch, low : low + step] = raw
        hidden_copy.wait()
        product = product + dot_nt(x_buf[:, low : low + step], rhs_buf[:, low : low + step])
        for index in range(blocks):
            rows = slice(index * block, (index + 1) * block)
            if part == 0:
                total = jnp.zeros((block, LANES), F32)
                for lane in range(0, step, LANES):
                    total = total + x_buf[rows, lane : lane + LANES].astype(F32)
                center = jnp.sum(total, axis=1, keepdims=True) * (1.0 / step)
                centers[index] = jnp.broadcast_to(center, (block, LANES))
            square = squares[index]
            for lane in range(low, low + step, LANES):
                gap = x_buf[rows, lane : lane + LANES].astype(F32) - centers[index]
                square = square + gap * gap
            squares[index] = square

    center = jnp.concatenate([value[:, 0:1] for value in centers], axis=0)
    spread = jnp.concatenate([jnp.sum(value, axis=1, keepdims=True) for value in squares], axis=0)
    average = product[0:tokens, 2 * patch : 2 * patch + 1] * (1.0 / width)
    spread = spread * (1.0 / width) - jnp.square(average - center)
    inverse = lax.rsqrt(spread + 1e-06)
    column_sum = product[tokens + 2 : tokens + 3, 0:patch]
    both = product[tokens : tokens + 1, :] + product[tokens + 1 : tokens + 2, :]
    offset_row = both[:, patch : 2 * patch]
    head = (product[0:tokens, 0:patch] - average * column_sum) * inverse + offset_row

    head_high, head_low = split_bf16(head)
    placed = dot_nn(one_hot, head_high) + dot_nn(one_hot, head_low)
    per = token_rows * token_cols
    for index in range(token_rows):
        pieces = [
            placed[f * per + index * token_cols : f * per + (index + 1) * token_cols, :]
            for f in range(frames)
        ]
        cells_buf[index] = jnp.concatenate(pieces, axis=1)

    slab_peers = (slab > 0).astype(jnp.int32) + (slab < slab_count - 1).astype(jnp.int32)
    seq_peers = (seq > 0).astype(jnp.int32) + (seq < seq_count - 1).astype(jnp.int32)
    pl.semaphore_wait(barrier, (1 + slab_peers) * (1 + seq_peers) - 1)

    pair = pltpu.make_async_remote_copy(
        src_ref=cells_buf.at[1 - half],
        dst_ref=partner_buf,
        send_sem=send_sem.at[0],
        recv_sem=recv_sem.at[0],
        device_id={"cfg": 1 - half},
        device_id_type=pl.DeviceIdType.MESH,
    )
    pair.start()

    small[-1].wait()
    position = 0
    for t in range(3):
        for shifted in range(2):
            for u in range(4):
                for e_in in range(2):
                    dx = (2 - 3 * e_in) if shifted else e_in
                    for e_out in range(2):
                        w = dx - e_out + 1
                        columns = slice(e_out * out_chan, (e_out + 1) * out_chan)
                        if u < 3 and 0 <= w <= 2:
                            value = conv_buf[(t * 3 + u) * 3 + w]
                        else:
                            value = jnp.zeros((chan, out_chan), BF16)
                        taps_buf[position : position + chan, columns] = value
                    position += chan

    pair.wait_recv()
    own = cells_buf[half]
    partner = partner_buf[...]
    cond = jnp.where(half == 0, own, partner)
    free = jnp.where(half == 0, partner, own)
    velocity = free + guidance_ref[0] * (cond - free)
    stepped = latent_buf[...] + step_size * velocity
    channels = stepped * std_row + mean_row
    high, low = split_bf16(channels)
    mixed = dot_nn(jnp.concatenate([high, low], axis=0), mix_both)
    mixed = mixed[0:token_cols, 0:LANES] + (
        mixed[0:token_cols, LANES:] + mixed[token_cols:, 0:LANES]
    )
    latent = (mixed + mix_row).astype(BF16)
    edge_buf[...] = latent

    copies = []
    for slot, (seq_step, slab_step) in enumerate(sends):
        copy = pltpu.make_async_remote_copy(
            src_ref=edge_buf,
            dst_ref=halo_buf.at[slot],
            send_sem=send_sem.at[1 + slot],
            recv_sem=recv_sem.at[1 + slot],
            device_id=place(seq_step, slab_step),
            device_id_type=pl.DeviceIdType.MESH,
        )
        copies.append(copy)
    for slot in (3, 4, 2, 0, 1):
        pl.when(present(*sends[slot]))(copies[slot].start)

    for slot, (seq_step, slab_step) in enumerate(sends):
        pl.when(present(-seq_step, -slab_step))(copies[slot].wait_recv)

    lane = lax.broadcasted_iota(jnp.int32, (token_cols, LANES), 1)
    line = lax.broadcasted_iota(jnp.int32, (token_cols, LANES), 0)
    odd = lax.rem(lax.div(lane, chan), 2) == 1

    def turned(value, amount):
        return pltpu.roll(value, amount % LANES, 1) if amount % LANES else value

    columns_of = []
    for center_block, above, below in (
        (halo_buf[2].astype(F32), halo_buf[3].astype(F32), halo_buf[4].astype(F32)),
        (latent.astype(F32), halo_buf[0].astype(F32), halo_buf[1].astype(F32)),
    ):
        for f in range(frames):
            base = f * 2 * span
            full = turned(center_block, span - base)
            full = jnp.where(lane < span, turned(above, -base - span), full)
            full = jnp.where(lane >= 3 * span, turned(below, 3 * span - base), full)
            before = jnp.where(line == 0, 0.0, pltpu.roll(full, 1, 0))
            after = jnp.where(line == token_cols - 1, 0.0, pltpu.roll(full, token_cols - 1, 0))
            beside = jnp.where(odd, before, after)
            lower = (turned(full, -span), turned(beside, -span))
            columns_of.append(
                (
                    (full.astype(BF16), beside.astype(BF16)),
                    (lower[0].astype(BF16), lower[1].astype(BF16)),
                )
            )
    taps = taps_buf[...]
    bias = conv_bias_buf[...]
    columns = jnp.concatenate(
        [
            jnp.concatenate(
                [piece for t in range(3) for piece in columns_of[f + t][y]], axis=1
            )
            for f in range(frames)
            for y in range(2)
        ],
        axis=0,
    )
    result = dot_nn(columns, taps)
    for f in range(frames):
        for y in range(2):
            first = (f * 2 + y) * token_cols
            for part in range(out_chan // LANES):
                lanes = slice(part * LANES, (part + 1) * LANES)
                for e in range(2):
                    from_lane = e * out_chan + part * LANES
                    wide_buf[part, pl.ds(2 * first + e, token_cols, stride=2), :] = (
                        result[first : first + token_cols, from_lane : from_lane + LANES]
                        + bias[part : part + 1, :]
                    )
                out_ref[f, y, :, lanes] = wide_buf[
                    part, 2 * first : 2 * first + 2 * token_cols, :
                ].astype(BF16)

    pair.wait_send()
    for slot in range(len(sends)):
        pl.when(present(*sends[slot]))(copies[slot].wait_send)


def per_device(
    counts,
    hidden,
    token_order,
    noisy_latent,
    head_weight,
    head_mod,
    guidance,
    timestep_index,
    step_table,
    vae_mean,
    vae_std,
    conv2_weight,
    conv2_bias,
    conv1_weight,
    conv1_bias,
):
    frames, lat_rows, lat_width = noisy_latent.shape
    chan = vae_mean.shape[0]
    tokens, width = hidden.shape[1:]
    patch = head_weight.shape[1]
    out_chan = conv1_weight.shape[2]
    token_cols = lat_width // (2 * chan)
    token_rows = lat_rows * counts[2] // 2
    chunks = 5
    operands = (
        hidden,
        token_order.reshape(1, -1),
        noisy_latent,
        head_weight.T,
        head_mod,
        guidance,
        timestep_index,
        step_table,
        vae_mean.reshape(1, -1),
        vae_std.reshape(1, -1),
        conv2_weight,
        conv2_bias.reshape(1, -1),
        conv1_weight,
        conv1_bias.reshape(-1, LANES),
    )
    block = (token_cols, LANES)
    scratch = [
        pltpu.VMEM((tokens + EXTRA, width), BF16),
        pltpu.VMEM((patch, width), BF16),
        pltpu.VMEM((2 * patch + EXTRA, width), BF16),
        pltpu.VMEM(operands[1].shape, jnp.int32),
        pltpu.VMEM(operands[2].shape, F32),
    ]
    scratch += [
        pltpu.VMEM(value.shape, value.dtype)
        for index, value in enumerate(operands)
        if index == 4 or index > 7
    ]
    scratch += [
        pltpu.VMEM((frames, lat_rows, lat_width // LANES, LANES), F32),
        pltpu.VMEM(block, F32),
        pltpu.VMEM((3 * 16 * chan, 2 * out_chan), BF16),
        pltpu.VMEM((token_rows,) + block, F32),
        pltpu.VMEM(block, F32),
        pltpu.VMEM(block, BF16),
        pltpu.VMEM((5,) + block, BF16),
        pltpu.VMEM((out_chan // LANES, frames * lat_rows * 2 * token_cols, LANES), F32),
        pltpu.SemaphoreType.DMA((9,)),
        pltpu.SemaphoreType.DMA((2, chunks)),
        pltpu.SemaphoreType.DMA((6,)),
        pltpu.SemaphoreType.DMA((6,)),
    ]
    sizes = tuple(counts) + (token_rows, token_cols, frames, chunks)
    return pl.pallas_call(
        functools.partial(kernel, sizes),
        out_shape=pltpu.VMEM((frames, lat_rows, 2 * token_cols, out_chan), BF16),
        in_specs=[
            pl.BlockSpec(memory_space=pltpu.SMEM if index in (5, 6, 7) else pl.ANY)
            for index in range(len(operands))
        ],
        out_specs=pl.BlockSpec(memory_space=pltpu.VMEM),
        scratch_shapes=scratch,
        compiler_params=pltpu.CompilerParams(
            collective_id=0, has_side_effects=True, vmem_limit_bytes=60 * 1024 * 1024
        ),
        name="guided_step",
    )(
        *[
            value
            if index in (5, 6, 7)
            else pltpu.with_memory_space_constraint(value, pltpu.HBM)
            for index, value in enumerate(operands)
        ]
    )


def solution(mesh):
    counts = (mesh.shape["seq"], mesh.shape["rows"], mesh.shape["cfg"])
    return jax.shard_map(
        functools.partial(per_device, counts),
        mesh=mesh,
        in_specs=(
            P("cfg", ("groups", "seq", "rows"), None),
            P(("groups", "seq", "rows")),
            P(("groups", "seq"), ("rows", "cfg"), None),
            P(),
            P(),
            P(),
            P(),
            P(),
            P(),
            P(),
            P(),
            P(),
            P(),
            P(),
        ),
        out_specs=P(("groups", "seq"), ("rows", "cfg"), None, None),
        check_vma=False,
    )
```

```python
import functools

import jax
import jax.numpy as jnp
from jax import lax
from jax.experimental import pallas as pl
from jax.experimental.pallas import tpu as pltpu
from jax.sharding import PartitionSpec as P

F32 = jnp.float32
BF16 = jnp.bfloat16
LANES = 128
EXTRA = 16


def split_bf16(value):
    high = value.astype(BF16)
    low = (value - high.astype(F32)).astype(BF16)
    return high, low


def dot_nt(left, right):
    return lax.dot_general(left, right, (((1,), (1,)), ((), ())), preferred_element_type=F32)


def dot_nn(left, right):
    return jnp.dot(left, right, preferred_element_type=F32)


def kernel(
    sizes,
    hidden_hbm,
    order_hbm,
    noisy_hbm,
    weight_hbm,
    mod_hbm,
    guidance_ref,
    index_ref,
    table_ref,
    mean_hbm,
    std_hbm,
    mix_hbm,
    mix_bias_hbm,
    conv_hbm,
    conv_bias_hbm,
    out_ref,
    x_buf,
    w_buf,
    rhs_buf,
    order_buf,
    noisy_buf,
    mod_buf,
    mean_buf,
    std_buf,
    mix_buf,
    mix_bias_buf,
    conv_buf,
    conv_bias_buf,
    lines_buf,
    latent_buf,
    taps_buf,
    cells_buf,
    partner_buf,
    center_buf,
    edge_buf,
    halo_buf,
    wide_buf,
    local_sem,
    chunk_sem,
    send_sem,
    recv_sem,
):
    seq_count, row_count, cfg_count, token_rows, token_cols, frames, chunks = sizes
    tokens = hidden_hbm.shape[1]
    width = hidden_hbm.shape[2]
    patch = weight_hbm.shape[0]
    chan = mix_hbm.shape[0]
    out_chan = conv_hbm.shape[2]
    slab_count = row_count * cfg_count
    step = width // chunks

    seq = lax.axis_index("seq")
    row = lax.axis_index("rows")
    half = lax.axis_index("cfg")
    slab = row * cfg_count + half

    small = []
    for source, target in (
        (mod_hbm, mod_buf),
        (order_hbm, order_buf),
        (noisy_hbm, noisy_buf),
        (mean_hbm, mean_buf),
        (std_hbm, std_buf),
        (mix_hbm, mix_buf),
        (mix_bias_hbm, mix_bias_buf),
        (conv_bias_hbm, conv_bias_buf),
        (conv_hbm, conv_buf),
    ):
        small.append(pltpu.make_async_copy(source, target, local_sem.at[len(small)]))
    loads = []
    weight_copy = pltpu.make_async_copy(weight_hbm, w_buf, chunk_sem.at[0])
    for part in range(chunks):
        columns = pl.ds(part * step, step)
        loads.append(
            pltpu.make_async_copy(
                hidden_hbm.at[0, :, columns],
                x_buf.at[pl.ds(0, tokens), columns],
                chunk_sem.at[1 + part],
            )
        )
    small[0].start()
    weight_copy.start()
    loads[0].start()
    for copy in small[1:-1]:
        copy.start()
    for copy in loads[1:]:
        copy.start()
    small[-1].start()

    barrier = pltpu.get_barrier_semaphore()

    def present(seq_step, slab_step):
        ok = jnp.bool_(True)
        if seq_step:
            ok = jnp.logical_and(ok, seq > 0 if seq_step < 0 else seq < seq_count - 1)
        if slab_step:
            ok = jnp.logical_and(ok, slab > 0 if slab_step < 0 else slab < slab_count - 1)
        return ok

    def place(seq_step, slab_step):
        other = slab + slab_step + cfg_count
        return {
            "seq": seq + seq_step,
            "rows": lax.div(other, cfg_count) - 1,
            "cfg": lax.rem(other, cfg_count),
        }

    around = [(a, b) for a in (-1, 0, 1) for b in (-1, 0, 1) if a or b]
    for offset in around:

        @pl.when(present(*offset))
        def _(offset=offset):
            pl.semaphore_signal(
                barrier, inc=1, device_id=place(*offset), device_id_type=pl.DeviceIdType.MESH
            )

    sends = ((0, 1), (0, -1), (1, 0), (1, 1), (1, -1))
    for slot, (seq_step, slab_step) in enumerate(sends):

        @pl.when(jnp.logical_not(present(-seq_step, -slab_step)))
        def _(slot=slot):
            if sends[slot][1]:
                halo_buf[slot] = jnp.zeros(halo_buf.shape[1:], BF16)
            else:
                center_buf[1] = jnp.zeros(center_buf.shape[1:], BF16)

    small[0].wait()
    scale = 1.0 + mod_buf[1:2, :]
    shift_high, shift_low = split_bf16(mod_buf[0:1, :])
    pick = lax.broadcasted_iota(jnp.int32, (EXTRA, width), 0)
    x_buf[tokens : tokens + EXTRA, :] = jnp.where(
        pick == 0,
        shift_high.astype(F32),
        jnp.where(pick == 1, shift_low.astype(F32), jnp.where(pick == 2, 1.0, 0.0)),
    ).astype(BF16)
    ones_row = lax.broadcasted_iota(jnp.int32, (EXTRA, width), 0) == 0
    rhs_buf[2 * patch : 2 * patch + EXTRA, :] = jnp.where(ones_row, 1.0, 0.0).astype(BF16)

    for copy in small[1:-1]:
        copy.wait()
    cell = order_buf[...].astype(F32) + 0.5
    per_frame = float(row_count * token_rows * token_cols)
    frame_all = jnp.floor(cell * (1.0 / per_frame))
    in_frame = cell - frame_all * per_frame
    frame_pos = frame_all - frames * jnp.floor((frame_all + 0.5) * (1.0 / frames))
    row_all = jnp.floor(in_frame * (1.0 / token_cols))
    column = in_frame - 0.5 - row_all * token_cols
    row_pos = row_all - token_rows * jnp.floor((row_all + 0.5) * (1.0 / token_rows))
    target = (frame_pos * token_rows + row_pos) * token_cols + column
    wanted = lax.broadcasted_iota(jnp.int32, (tokens, tokens), 0).astype(F32)
    one_hot = jnp.where(jnp.abs(wanted - target) < 0.25, 1.0, 0.0).astype(BF16)
    for f in range(frames):
        for a in range(2):
            for g in range(lines_buf.shape[2]):
                lines_buf[f, a, g : g + 1, :] = noisy_buf[f, a : a + 1, g * LANES : (g + 1) * LANES]
    lane = lax.broadcasted_iota(jnp.int32, (lines_buf.shape[2], LANES), 1)
    span = 2 * chan
    per_line = LANES // span
    groups = lines_buf.shape[2]
    for jj in range(per_line):
        line = jnp.zeros((groups, LANES), F32)
        for f in range(frames):
            for a in range(2):
                slot = f * 2 + a
                moved = lines_buf[f, a]
                if (slot - jj) % per_line:
                    moved = pltpu.roll(moved, ((slot - jj) * span) % LANES, 1)
                line = jnp.where((lane >= slot * span) & (lane < (slot + 1) * span), moved, line)
        latent_buf[pl.ds(jj, groups, stride=per_line), :] = line

    repeat = LANES // chan

    def lanes_of(ref):
        return jnp.concatenate([ref[...]] * repeat, axis=1)

    mean_row = lanes_of(mean_buf)
    std_row = lanes_of(std_buf)
    mix_row = lanes_of(mix_bias_buf)
    mix = jnp.concatenate([lanes_of(mix_buf)] * repeat, axis=0)
    mix_in = lax.broadcasted_iota(jnp.int32, (LANES, LANES), 0)
    mix_out = lax.broadcasted_iota(jnp.int32, (LANES, LANES), 1)
    group_in = lax.div(mix_in, chan)
    wanted_out = (
        lax.rem(lax.div(group_in, 2), 2) * (2 * frames)
        + lax.div(group_in, 4) * 2
        + lax.rem(group_in, 2)
    )
    same = wanted_out == lax.div(mix_out, chan)
    mix_high, mix_low = split_bf16(jnp.where(same, mix, 0.0))
    mix_both = jnp.concatenate([mix_high, mix_low], axis=1)

    at = index_ref[0]
    now = jnp.full((1, LANES), table_ref[at].astype(F32))
    later = jnp.full((1, LANES), table_ref[at + 1].astype(F32))
    step_size = later / 1000.0 - now / 1000.0

    weight_copy.wait()
    rhs_buf[0:patch, :] = (w_buf[...].astype(F32) * scale).astype(BF16)
    rhs_buf[patch : 2 * patch, :] = w_buf[...]

    block = 64
    blocks = tokens // block
    product = jnp.zeros((tokens + EXTRA, rhs_buf.shape[0]), F32)
    centers = [None] * blocks
    squares = [jnp.zeros((block, LANES), F32)] * blocks
    for part, hidden_copy in enumerate(loads):
        low = part * step
        hidden_copy.wait()
        product = product + dot_nt(x_buf[:, low : low + step], rhs_buf[:, low : low + step])
        for index in range(blocks):
            rows = slice(index * block, (index + 1) * block)
            if part == 0:
                total = jnp.zeros((block, LANES), F32)
                for lane in range(0, step, LANES):
                    total = total + x_buf[rows, lane : lane + LANES].astype(F32)
                center = jnp.sum(total, axis=1, keepdims=True) * (1.0 / step)
                centers[index] = jnp.broadcast_to(center, (block, LANES))
            square = squares[index]
            for lane in range(low, low + step, LANES):
                gap = x_buf[rows, lane : lane + LANES].astype(F32) - centers[index]
                square = square + gap * gap
            squares[index] = square

    center = jnp.concatenate([value[:, 0:1] for value in centers], axis=0)
    spread = jnp.concatenate([jnp.sum(value, axis=1, keepdims=True) for value in squares], axis=0)
    average = product[0:tokens, 2 * patch : 2 * patch + 1] * (1.0 / width)
    spread = spread * (1.0 / width) - jnp.square(average - center)
    inverse = lax.rsqrt(spread + 1e-06)
    column_sum = product[tokens + 2 : tokens + 3, 0:patch]
    both = product[tokens : tokens + 1, :] + product[tokens + 1 : tokens + 2, :]
    offset_row = both[:, patch : 2 * patch]
    head = (product[0:tokens, 0:patch] - average * column_sum) * inverse + offset_row

    head_high, head_low = split_bf16(head)
    placed = dot_nn(one_hot, head_high) + dot_nn(one_hot, head_low)
    per = token_rows * token_cols
    for index in range(token_rows):
        pieces = [
            placed[f * per + index * token_cols : f * per + (index + 1) * token_cols, :]
            for f in range(frames)
        ]
        cells_buf[index] = jnp.concatenate(pieces, axis=1)

    slab_peers = (slab > 0).astype(jnp.int32) + (slab < slab_count - 1).astype(jnp.int32)
    seq_peers = (seq > 0).astype(jnp.int32) + (seq < seq_count - 1).astype(jnp.int32)
    pl.semaphore_wait(barrier, (1 + slab_peers) * (1 + seq_peers) - 1)

    pair = pltpu.make_async_remote_copy(
        src_ref=cells_buf.at[1 - half],
        dst_ref=partner_buf,
        send_sem=send_sem.at[0],
        recv_sem=recv_sem.at[0],
        device_id={"cfg": 1 - half},
        device_id_type=pl.DeviceIdType.MESH,
    )
    pair.start()

    small[-1].wait()
    position = 0
    for t in range(3):
        for shifted in range(2):
            for u in range(4):
                for e_in in range(2):
                    dx = (2 - 3 * e_in) if shifted else e_in
                    for e_out in range(2):
                        w = dx - e_out + 1
                        columns = slice(e_out * out_chan, (e_out + 1) * out_chan)
                        if u < 3 and 0 <= w <= 2:
                            value = conv_buf[(t * 3 + u) * 3 + w]
                        else:
                            value = jnp.zeros((chan, out_chan), BF16)
                        taps_buf[position : position + chan, columns] = value
                    position += chan

    pair.wait_recv()
    own = cells_buf[half]
    partner = partner_buf[...]
    cond = jnp.where(half == 0, own, partner)
    free = jnp.where(half == 0, partner, own)
    velocity = free + guidance_ref[0] * (cond - free)
    stepped = latent_buf[...] + step_size * velocity
    channels = stepped * std_row + mean_row
    high, low = split_bf16(channels)
    mixed = dot_nn(jnp.concatenate([high, low], axis=0), mix_both)
    mixed = mixed[0:token_cols, 0:LANES] + (
        mixed[0:token_cols, LANES:] + mixed[token_cols:, 0:LANES]
    )
    latent = (mixed + mix_row).astype(BF16)
    exact = latent.astype(F32)
    fold = token_cols // 2
    left = lax.broadcasted_iota(jnp.int32, (fold, LANES), 1) < LANES // 2
    first, second = exact[0:fold], exact[fold:]
    edge_buf[0] = jnp.where(left, first, pltpu.roll(second, LANES // 2, 1)).astype(BF16)
    edge_buf[1] = jnp.where(left, pltpu.roll(first, LANES // 2, 1), second).astype(BF16)
    center_buf[0] = latent

    copies = []
    for slot, (seq_step, slab_step) in enumerate(sends):
        if slab_step:
            source, target = edge_buf.at[(1 + slab_step) // 2], halo_buf.at[slot]
        else:
            source, target = center_buf.at[0], center_buf.at[1]
        copy = pltpu.make_async_remote_copy(
            src_ref=source,
            dst_ref=target,
            send_sem=send_sem.at[1 + slot],
            recv_sem=recv_sem.at[1 + slot],
            device_id=place(seq_step, slab_step),
            device_id_type=pl.DeviceIdType.MESH,
        )
        copies.append(copy)
    for slot in (3, 4, 2, 0, 1):
        pl.when(present(*sends[slot]))(copies[slot].start)

    for slot, (seq_step, slab_step) in enumerate(sends):
        pl.when(present(-seq_step, -slab_step))(copies[slot].wait_recv)

    lane = lax.broadcasted_iota(jnp.int32, (token_cols, LANES), 1)
    line = lax.broadcasted_iota(jnp.int32, (token_cols, LANES), 0)
    odd = lax.rem(lax.div(lane, chan), 2) == 1

    def turned(value, amount):
        return pltpu.roll(value, amount % LANES, 1) if amount % LANES else value

    def spread_rows(block, f, lane_base):
        return jnp.concatenate(
            [turned(block, lane_base - (part * frames + f) * span) for part in range(2)], axis=0
        )

    columns_of = []
    for center_block, above, below in (
        (center_buf[1].astype(F32), halo_buf[3].astype(F32), halo_buf[4].astype(F32)),
        (exact, halo_buf[0].astype(F32), halo_buf[1].astype(F32)),
    ):
        for f in range(frames):
            full = turned(center_block, span - f * span)
            full = jnp.where(lane >= 2 * span, turned(center_block, -f * span), full)
            full = jnp.where(lane < span, spread_rows(above, f, 0), full)
            full = jnp.where(lane >= 3 * span, spread_rows(below, f, 3 * span), full)
            before = jnp.where(line == 0, 0.0, pltpu.roll(full, 1, 0))
            after = jnp.where(line == token_cols - 1, 0.0, pltpu.roll(full, token_cols - 1, 0))
            beside = jnp.where(odd, before, after)
            lower = (turned(full, -span), turned(beside, -span))
            columns_of.append(
                (
                    (full.astype(BF16), beside.astype(BF16)),
                    (lower[0].astype(BF16), lower[1].astype(BF16)),
                )
            )
    taps = taps_buf[...]
    bias = conv_bias_buf[...]
    columns = jnp.concatenate(
        [
            jnp.concatenate(
                [piece for t in range(3) for piece in columns_of[f + t][y]], axis=1
            )
            for f in range(frames)
            for y in range(2)
        ],
        axis=0,
    )
    result = dot_nn(columns, taps)
    for f in range(frames):
        for y in range(2):
            first = (f * 2 + y) * token_cols
            for part in range(out_chan // LANES):
                lanes = slice(part * LANES, (part + 1) * LANES)
                for e in range(2):
                    from_lane = e * out_chan + part * LANES
                    wide_buf[part, pl.ds(2 * first + e, token_cols, stride=2), :] = (
                        result[first : first + token_cols, from_lane : from_lane + LANES]
                        + bias[part : part + 1, :]
                    )
                out_ref[f, y, :, lanes] = wide_buf[
                    part, 2 * first : 2 * first + 2 * token_cols, :
                ].astype(BF16)

    pair.wait_send()
    for slot in range(len(sends)):
        pl.when(present(*sends[slot]))(copies[slot].wait_send)


def per_device(
    counts,
    hidden,
    token_order,
    noisy_latent,
    head_weight,
    head_mod,
    guidance,
    timestep_index,
    step_table,
    vae_mean,
    vae_std,
    conv2_weight,
    conv2_bias,
    conv1_weight,
    conv1_bias,
):
    frames, lat_rows, lat_width = noisy_latent.shape
    chan = vae_mean.shape[0]
    tokens, width = hidden.shape[1:]
    patch = head_weight.shape[1]
    out_chan = conv1_weight.shape[2]
    token_cols = lat_width // (2 * chan)
    token_rows = lat_rows * counts[2] // 2
    chunks = 5
    operands = (
        hidden,
        token_order.reshape(1, -1),
        noisy_latent,
        head_weight.T,
        head_mod,
        guidance,
        timestep_index,
        step_table,
        vae_mean.reshape(1, -1),
        vae_std.reshape(1, -1),
        conv2_weight,
        conv2_bias.reshape(1, -1),
        conv1_weight,
        conv1_bias.reshape(-1, LANES),
    )
    block = (token_cols, LANES)
    scratch = [
        pltpu.VMEM((tokens + EXTRA, width), BF16),
        pltpu.VMEM((patch, width), BF16),
        pltpu.VMEM((2 * patch + EXTRA, width), BF16),
        pltpu.VMEM(operands[1].shape, jnp.int32),
        pltpu.VMEM(operands[2].shape, F32),
    ]
    scratch += [
        pltpu.VMEM(value.shape, value.dtype)
        for index, value in enumerate(operands)
        if index == 4 or index > 7
    ]
    scratch += [
        pltpu.VMEM((frames, lat_rows, lat_width // LANES, LANES), F32),
        pltpu.VMEM(block, F32),
        pltpu.VMEM((3 * 16 * chan, 2 * out_chan), BF16),
        pltpu.VMEM((token_rows,) + block, F32),
        pltpu.VMEM(block, F32),
        pltpu.VMEM((2,) + block, BF16),
        pltpu.VMEM((2, token_cols // 2, LANES), BF16),
        pltpu.VMEM((5, token_cols // 2, LANES), BF16),
        pltpu.VMEM((out_chan // LANES, frames * lat_rows * 2 * token_cols, LANES), F32),
        pltpu.SemaphoreType.DMA((9,)),
        pltpu.SemaphoreType.DMA((1 + chunks,)),
        pltpu.SemaphoreType.DMA((6,)),
        pltpu.SemaphoreType.DMA((6,)),
    ]
    sizes = tuple(counts) + (token_rows, token_cols, frames, chunks)
    return pl.pallas_call(
        functools.partial(kernel, sizes),
        out_shape=pltpu.VMEM((frames, lat_rows, 2 * token_cols, out_chan), BF16),
        in_specs=[
            pl.BlockSpec(memory_space=pltpu.SMEM if index in (5, 6, 7) else pl.ANY)
            for index in range(len(operands))
        ],
        out_specs=pl.BlockSpec(memory_space=pltpu.VMEM),
        scratch_shapes=scratch,
        compiler_params=pltpu.CompilerParams(
            collective_id=0, has_side_effects=True, vmem_limit_bytes=60 * 1024 * 1024
        ),
        name="guided_step",
    )(
        *[
            value
            if index in (5, 6, 7)
            else pltpu.with_memory_space_constraint(value, pltpu.HBM)
            for index, value in enumerate(operands)
        ]
    )


def solution(mesh):
    counts = (mesh.shape["seq"], mesh.shape["rows"], mesh.shape["cfg"])
    return jax.shard_map(
        functools.partial(per_device, counts),
        mesh=mesh,
        in_specs=(
            P("cfg", ("groups", "seq", "rows"), None),
            P(("groups", "seq", "rows")),
            P(("groups", "seq"), ("rows", "cfg"), None),
            P(),
            P(),
            P(),
            P(),
            P(),
            P(),
            P(),
            P(),
            P(),
            P(),
            P(),
        ),
        out_specs=P(("groups", "seq"), ("rows", "cfg"), None, None),
        check_vma=False,
    )
```

```python
import functools

import jax
import jax.numpy as jnp
from jax import lax
from jax.experimental import pallas as pl
from jax.experimental.pallas import tpu as pltpu
from jax.sharding import PartitionSpec as P

F32 = jnp.float32
BF16 = jnp.bfloat16
LANES = 128
EXTRA = 16


def split_bf16(value):
    high = value.astype(BF16)
    low = (value - high.astype(F32)).astype(BF16)
    return high, low


def dot_nt(left, right):
    return lax.dot_general(left, right, (((1,), (1,)), ((), ())), preferred_element_type=F32)


def dot_nn(left, right):
    return jnp.dot(left, right, preferred_element_type=F32)


def kernel(
    sizes,
    hidden_hbm,
    order_hbm,
    noisy_hbm,
    weight_hbm,
    mod_hbm,
    guidance_ref,
    index_ref,
    table_ref,
    mean_hbm,
    std_hbm,
    mix_hbm,
    mix_bias_hbm,
    conv_hbm,
    conv_bias_hbm,
    out_ref,
    x_buf,
    w_buf,
    rhs_buf,
    order_buf,
    noisy_buf,
    mod_buf,
    mean_buf,
    std_buf,
    mix_buf,
    mix_bias_buf,
    conv_buf,
    conv_bias_buf,
    lines_buf,
    latent_buf,
    taps_buf,
    cells_buf,
    partner_buf,
    center_buf,
    edge_buf,
    halo_buf,
    wide_buf,
    local_sem,
    chunk_sem,
    send_sem,
    recv_sem,
):
    seq_count, row_count, cfg_count, token_rows, token_cols, frames, chunks = sizes
    tokens = hidden_hbm.shape[1]
    width = hidden_hbm.shape[2]
    patch = weight_hbm.shape[0]
    chan = mix_hbm.shape[0]
    out_chan = conv_hbm.shape[2]
    slab_count = row_count * cfg_count
    step = width // chunks

    seq = lax.axis_index("seq")
    row = lax.axis_index("rows")
    half = lax.axis_index("cfg")
    slab = row * cfg_count + half

    small = []
    for source, target in (
        (mod_hbm, mod_buf),
        (order_hbm, order_buf),
        (noisy_hbm, noisy_buf),
        (mean_hbm, mean_buf),
        (std_hbm, std_buf),
        (mix_hbm, mix_buf),
        (mix_bias_hbm, mix_bias_buf),
        (conv_bias_hbm, conv_bias_buf),
        (conv_hbm, conv_buf),
    ):
        small.append(pltpu.make_async_copy(source, target, local_sem.at[len(small)]))
    loads = []
    weight_copy = pltpu.make_async_copy(weight_hbm, w_buf, chunk_sem.at[0])
    for part in range(chunks):
        columns = pl.ds(part * step, step)
        loads.append(
            pltpu.make_async_copy(
                hidden_hbm.at[0, :, columns],
                x_buf.at[:, columns],
                chunk_sem.at[1 + part],
            )
        )
    small[0].start()
    weight_copy.start()
    loads[0].start()
    for copy in small[1:-1]:
        copy.start()
    for copy in loads[1:]:
        copy.start()
    small[-1].start()

    barrier = pltpu.get_barrier_semaphore()

    def present(seq_step, slab_step):
        ok = jnp.bool_(True)
        if seq_step:
            ok = jnp.logical_and(ok, seq > 0 if seq_step < 0 else seq < seq_count - 1)
        if slab_step:
            ok = jnp.logical_and(ok, slab > 0 if slab_step < 0 else slab < slab_count - 1)
        return ok

    def place(seq_step, slab_step):
        other = slab + slab_step + cfg_count
        return {
            "seq": seq + seq_step,
            "rows": lax.div(other, cfg_count) - 1,
            "cfg": lax.rem(other, cfg_count),
        }

    around = [(a, b) for a in (-1, 0, 1) for b in (-1, 0, 1) if a or b]
    for offset in around:

        @pl.when(present(*offset))
        def _(offset=offset):
            pl.semaphore_signal(
                barrier, inc=1, device_id=place(*offset), device_id_type=pl.DeviceIdType.MESH
            )

    sends = ((0, 1), (0, -1), (1, 0), (1, 1), (1, -1))
    for slot, (seq_step, slab_step) in enumerate(sends):

        @pl.when(jnp.logical_not(present(-seq_step, -slab_step)))
        def _(slot=slot):
            if sends[slot][1]:
                halo_buf[slot] = jnp.zeros(halo_buf.shape[1:], BF16)
            else:
                center_buf[1] = jnp.zeros(center_buf.shape[1:], BF16)

    small[0].wait()
    scale = 1.0 + mod_buf[1:2, :]
    ones_row = lax.broadcasted_iota(jnp.int32, (EXTRA, width), 0) == 0
    rhs_buf[patch : patch + EXTRA, :] = jnp.where(ones_row, 1.0, 0.0).astype(BF16)

    for copy in small[1:-1]:
        copy.wait()
    cell = order_buf[...].astype(F32) + 0.5
    per_frame = float(row_count * token_rows * token_cols)
    frame_all = jnp.floor(cell * (1.0 / per_frame))
    in_frame = cell - frame_all * per_frame
    frame_pos = frame_all - frames * jnp.floor((frame_all + 0.5) * (1.0 / frames))
    row_all = jnp.floor(in_frame * (1.0 / token_cols))
    column = in_frame - 0.5 - row_all * token_cols
    row_pos = row_all - token_rows * jnp.floor((row_all + 0.5) * (1.0 / token_rows))
    target = (frame_pos * token_rows + row_pos) * token_cols + column
    wanted = lax.broadcasted_iota(jnp.int32, (tokens, tokens), 0).astype(F32)
    one_hot = jnp.where(jnp.abs(wanted - target) < 0.25, 1.0, 0.0).astype(BF16)
    weight_copy.wait()
    column_part = jnp.zeros((patch, LANES), F32)
    offset_part = jnp.zeros((patch, LANES), F32)
    for lane in range(0, width, LANES):
        lanes = slice(lane, lane + LANES)
        raw = w_buf[:, lanes].astype(F32)
        scaled = (raw * scale[:, lanes]).astype(BF16)
        rhs_buf[0:patch, lanes] = scaled
        column_part = column_part + scaled.astype(F32)
        offset_part = offset_part + raw * mod_buf[0:1, lanes]
    rest = jnp.concatenate([column_part, offset_part], axis=0)
    ones = jnp.ones((EXTRA, LANES), BF16)
    sums = jnp.zeros((EXTRA, 2 * patch), F32)
    for _ in range(3):
        piece = rest.astype(BF16)
        rest = rest - piece.astype(F32)
        sums = sums + dot_nt(ones, piece)
    column_sum = sums[0:1, 0:patch]
    offset_row = sums[0:1, patch:]

    block = 64
    blocks = tokens // block
    product = jnp.zeros((tokens, rhs_buf.shape[0]), F32)
    centers = [None] * blocks
    squares = [jnp.zeros((block, LANES), F32)] * blocks
    for part, hidden_copy in enumerate(loads):
        low = part * step
        hidden_copy.wait()
        product = product + dot_nt(x_buf[:, low : low + step], rhs_buf[:, low : low + step])
        for index in range(blocks):
            rows = slice(index * block, (index + 1) * block)
            if part == 0:
                total = x_buf[rows, 0:LANES].astype(F32)
                center = jnp.sum(total, axis=1, keepdims=True) * (1.0 / LANES)
                centers[index] = jnp.broadcast_to(center, (block, LANES))
            square = squares[index]
            for lane in range(low, low + step, LANES):
                gap = x_buf[rows, lane : lane + LANES].astype(F32) - centers[index]
                square = square + gap * gap
            squares[index] = square

    center = jnp.concatenate([value[:, 0:1] for value in centers], axis=0)
    spread = jnp.concatenate([jnp.sum(value, axis=1, keepdims=True) for value in squares], axis=0)
    average = product[:, patch : patch + 1] * (1.0 / width)
    spread = spread * (1.0 / width) - jnp.square(average - center)
    inverse = lax.rsqrt(spread + 1e-06)
    head = (product[:, 0:patch] - average * column_sum) * inverse + offset_row

    head_high, head_low = split_bf16(head)
    placed = dot_nn(one_hot, jnp.concatenate([head_high, head_low], axis=1))
    placed = placed[:, 0:patch] + placed[:, patch:]
    per = token_rows * token_cols
    for index in range(token_rows):
        pieces = [
            placed[f * per + index * token_cols : f * per + (index + 1) * token_cols, :]
            for f in range(frames)
        ]
        cells_buf[index] = jnp.concatenate(pieces, axis=1)

    slab_peers = (slab > 0).astype(jnp.int32) + (slab < slab_count - 1).astype(jnp.int32)
    seq_peers = (seq > 0).astype(jnp.int32) + (seq < seq_count - 1).astype(jnp.int32)
    pl.semaphore_wait(barrier, (1 + slab_peers) * (1 + seq_peers) - 1)

    pair = pltpu.make_async_remote_copy(
        src_ref=cells_buf.at[1 - half],
        dst_ref=partner_buf,
        send_sem=send_sem.at[0],
        recv_sem=recv_sem.at[0],
        device_id={"cfg": 1 - half},
        device_id_type=pl.DeviceIdType.MESH,
    )
    pair.start()

    for f in range(frames):
        for a in range(2):
            for g in range(lines_buf.shape[2]):
                lines_buf[f, a, g : g + 1, :] = noisy_buf[f, a : a + 1, g * LANES : (g + 1) * LANES]
    lane = lax.broadcasted_iota(jnp.int32, (lines_buf.shape[2], LANES), 1)
    span = 2 * chan
    per_line = LANES // span
    groups = lines_buf.shape[2]
    for jj in range(per_line):
        line = jnp.zeros((groups, LANES), F32)
        for f in range(frames):
            for a in range(2):
                slot = f * 2 + a
                moved = lines_buf[f, a]
                if (slot - jj) % per_line:
                    moved = pltpu.roll(moved, ((slot - jj) * span) % LANES, 1)
                line = jnp.where((lane >= slot * span) & (lane < (slot + 1) * span), moved, line)
        latent_buf[pl.ds(jj, groups, stride=per_line), :] = line

    repeat = LANES // chan

    def lanes_of(ref):
        return jnp.concatenate([ref[...]] * repeat, axis=1)

    mean_row = lanes_of(mean_buf)
    std_row = lanes_of(std_buf)
    mix_row = lanes_of(mix_bias_buf)
    mix = jnp.concatenate([lanes_of(mix_buf)] * repeat, axis=0)
    mix_in = lax.broadcasted_iota(jnp.int32, (LANES, LANES), 0)
    mix_out = lax.broadcasted_iota(jnp.int32, (LANES, LANES), 1)
    group_in = lax.div(mix_in, chan)
    wanted_out = (
        lax.rem(lax.div(group_in, 2), 2) * (2 * frames)
        + lax.div(group_in, 4) * 2
        + lax.rem(group_in, 2)
    )
    same = wanted_out == lax.div(mix_out, chan)
    mix_high, mix_low = split_bf16(jnp.where(same, mix, 0.0))
    mix_both = jnp.concatenate([mix_high, mix_low], axis=1)

    at = index_ref[0]
    now = jnp.full((1, LANES), table_ref[at].astype(F32))
    later = jnp.full((1, LANES), table_ref[at + 1].astype(F32))
    step_size = later / 1000.0 - now / 1000.0

    small[-1].wait()
    position = 0
    for t in range(3):
        for shifted in range(2):
            for u in range(4):
                for e_in in range(2):
                    dx = (2 - 3 * e_in) if shifted else e_in
                    for e_out in range(2):
                        w = dx - e_out + 1
                        columns = slice(e_out * out_chan, (e_out + 1) * out_chan)
                        if u < 3 and 0 <= w <= 2:
                            value = conv_buf[(t * 3 + u) * 3 + w]
                        else:
                            value = jnp.zeros((chan, out_chan), BF16)
                        taps_buf[position : position + chan, columns] = value
                    position += chan

    pair.wait_recv()
    own = cells_buf[half]
    partner = partner_buf[...]
    cond = jnp.where(half == 0, own, partner)
    free = jnp.where(half == 0, partner, own)
    velocity = free + guidance_ref[0] * (cond - free)
    stepped = latent_buf[...] + step_size * velocity
    channels = stepped * std_row + mean_row
    high, low = split_bf16(channels)
    mixed = dot_nn(jnp.concatenate([high, low], axis=0), mix_both)
    mixed = mixed[0:token_cols, 0:LANES] + (
        mixed[0:token_cols, LANES:] + mixed[token_cols:, 0:LANES]
    )
    latent = (mixed + mix_row).astype(BF16)
    exact = latent.astype(F32)
    fold = token_cols // 2
    left = lax.broadcasted_iota(jnp.int32, (fold, LANES), 1) < LANES // 2
    first, second = exact[0:fold], exact[fold:]
    edge_buf[0] = jnp.where(left, first, pltpu.roll(second, LANES // 2, 1)).astype(BF16)
    edge_buf[1] = jnp.where(left, pltpu.roll(first, LANES // 2, 1), second).astype(BF16)
    center_buf[0] = latent

    copies = []
    for slot, (seq_step, slab_step) in enumerate(sends):
        if slab_step:
            source, target = edge_buf.at[(1 + slab_step) // 2], halo_buf.at[slot]
        else:
            source, target = center_buf.at[0], center_buf.at[1]
        copy = pltpu.make_async_remote_copy(
            src_ref=source,
            dst_ref=target,
            send_sem=send_sem.at[1 + slot],
            recv_sem=recv_sem.at[1 + slot],
            device_id=place(seq_step, slab_step),
            device_id_type=pl.DeviceIdType.MESH,
        )
        copies.append(copy)
    for slot in (3, 4, 2, 0, 1):
        pl.when(present(*sends[slot]))(copies[slot].start)

    for slot, (seq_step, slab_step) in enumerate(sends):
        pl.when(present(-seq_step, -slab_step))(copies[slot].wait_recv)

    lane = lax.broadcasted_iota(jnp.int32, (token_cols, LANES), 1)
    line = lax.broadcasted_iota(jnp.int32, (token_cols, LANES), 0)
    odd = lax.rem(lax.div(lane, chan), 2) == 1

    def turned(value, amount):
        return pltpu.roll(value, amount % LANES, 1) if amount % LANES else value

    def spread_rows(block, f, lane_base):
        return jnp.concatenate(
            [turned(block, lane_base - (part * frames + f) * span) for part in range(2)], axis=0
        )

    columns_of = []
    for center_block, above, below in (
        (center_buf[1].astype(F32), halo_buf[3].astype(F32), halo_buf[4].astype(F32)),
        (exact, halo_buf[0].astype(F32), halo_buf[1].astype(F32)),
    ):
        for f in range(frames):
            full = turned(center_block, span - f * span)
            full = jnp.where(lane >= 2 * span, turned(center_block, -f * span), full)
            full = jnp.where(lane < span, spread_rows(above, f, 0), full)
            full = jnp.where(lane >= 3 * span, spread_rows(below, f, 3 * span), full)
            before = jnp.where(line == 0, 0.0, pltpu.roll(full, 1, 0))
            after = jnp.where(line == token_cols - 1, 0.0, pltpu.roll(full, token_cols - 1, 0))
            beside = jnp.where(odd, before, after)
            lower = (turned(full, -span), turned(beside, -span))
            columns_of.append(
                (
                    (full.astype(BF16), beside.astype(BF16)),
                    (lower[0].astype(BF16), lower[1].astype(BF16)),
                )
            )
    taps = taps_buf[...]
    bias = conv_bias_buf[...]
    columns = jnp.concatenate(
        [
            jnp.concatenate(
                [piece for t in range(3) for piece in columns_of[f + t][y]], axis=1
            )
            for f in range(frames)
            for y in range(2)
        ],
        axis=0,
    )
    result = dot_nn(columns, taps)
    for f in range(frames):
        for y in range(2):
            first = (f * 2 + y) * token_cols
            for part in range(out_chan // LANES):
                lanes = slice(part * LANES, (part + 1) * LANES)
                for e in range(2):
                    from_lane = e * out_chan + part * LANES
                    wide_buf[part, pl.ds(2 * first + e, token_cols, stride=2), :] = (
                        result[first : first + token_cols, from_lane : from_lane + LANES]
                        + bias[part : part + 1, :]
                    )
                out_ref[f, y, :, lanes] = wide_buf[
                    part, 2 * first : 2 * first + 2 * token_cols, :
                ].astype(BF16)

    pair.wait_send()
    for slot in range(len(sends)):
        pl.when(present(*sends[slot]))(copies[slot].wait_send)


def per_device(
    counts,
    hidden,
    token_order,
    noisy_latent,
    head_weight,
    head_mod,
    guidance,
    timestep_index,
    step_table,
    vae_mean,
    vae_std,
    conv2_weight,
    conv2_bias,
    conv1_weight,
    conv1_bias,
):
    frames, lat_rows, lat_width = noisy_latent.shape
    chan = vae_mean.shape[0]
    tokens, width = hidden.shape[1:]
    patch = head_weight.shape[1]
    out_chan = conv1_weight.shape[2]
    token_cols = lat_width // (2 * chan)
    token_rows = lat_rows * counts[2] // 2
    chunks = 5
    operands = (
        hidden,
        token_order.reshape(1, -1),
        noisy_latent,
        head_weight.T,
        head_mod,
        guidance,
        timestep_index,
        step_table,
        vae_mean.reshape(1, -1),
        vae_std.reshape(1, -1),
        conv2_weight,
        conv2_bias.reshape(1, -1),
        conv1_weight,
        conv1_bias.reshape(-1, LANES),
    )
    block = (token_cols, LANES)
    scratch = [
        pltpu.VMEM((tokens, width), BF16),
        pltpu.VMEM((patch, width), BF16),
        pltpu.VMEM((patch + EXTRA, width), BF16),
        pltpu.VMEM(operands[1].shape, jnp.int32),
        pltpu.VMEM(operands[2].shape, F32),
    ]
    scratch += [
        pltpu.VMEM(value.shape, value.dtype)
        for index, value in enumerate(operands)
        if index == 4 or index > 7
    ]
    scratch += [
        pltpu.VMEM((frames, lat_rows, lat_width // LANES, LANES), F32),
        pltpu.VMEM(block, F32),
        pltpu.VMEM((3 * 16 * chan, 2 * out_chan), BF16),
        pltpu.VMEM((token_rows,) + block, F32),
        pltpu.VMEM(block, F32),
        pltpu.VMEM((2,) + block, BF16),
        pltpu.VMEM((2, token_cols // 2, LANES), BF16),
        pltpu.VMEM((5, token_cols // 2, LANES), BF16),
        pltpu.VMEM((out_chan // LANES, frames * lat_rows * 2 * token_cols, LANES), F32),
        pltpu.SemaphoreType.DMA((9,)),
        pltpu.SemaphoreType.DMA((1 + chunks,)),
        pltpu.SemaphoreType.DMA((6,)),
        pltpu.SemaphoreType.DMA((6,)),
    ]
    sizes = tuple(counts) + (token_rows, token_cols, frames, chunks)
    return pl.pallas_call(
        functools.partial(kernel, sizes),
        out_shape=pltpu.VMEM((frames, lat_rows, 2 * token_cols, out_chan), BF16),
        in_specs=[
            pl.BlockSpec(memory_space=pltpu.SMEM if index in (5, 6, 7) else pl.ANY)
            for index in range(len(operands))
        ],
        out_specs=pl.BlockSpec(memory_space=pltpu.VMEM),
        scratch_shapes=scratch,
        compiler_params=pltpu.CompilerParams(
            collective_id=0, has_side_effects=True, vmem_limit_bytes=60 * 1024 * 1024
        ),
        name="guided_step",
    )(
        *[
            value
            if index in (5, 6, 7)
            else pltpu.with_memory_space_constraint(value, pltpu.HBM)
            for index, value in enumerate(operands)
        ]
    )


def solution(mesh):
    counts = (mesh.shape["seq"], mesh.shape["rows"], mesh.shape["cfg"])
    return jax.shard_map(
        functools.partial(per_device, counts),
        mesh=mesh,
        in_specs=(
            P("cfg", ("groups", "seq", "rows"), None),
            P(("groups", "seq", "rows")),
            P(("groups", "seq"), ("rows", "cfg"), None),
            P(),
            P(),
            P(),
            P(),
            P(),
            P(),
            P(),
            P(),
            P(),
            P(),
            P(),
        ),
        out_specs=P(("groups", "seq"), ("rows", "cfg"), None, None),
        check_vma=False,
    )
```

```python
import functools

import jax
import jax.numpy as jnp
from jax import lax
from jax.experimental import pallas as pl
from jax.experimental.pallas import tpu as pltpu
from jax.sharding import PartitionSpec as P

F32 = jnp.float32
BF16 = jnp.bfloat16
LANES = 128
EXTRA = 16


def split_bf16(value):
    high = value.astype(BF16)
    low = (value - high.astype(F32)).astype(BF16)
    return high, low


def dot_nt(left, right):
    return lax.dot_general(left, right, (((1,), (1,)), ((), ())), preferred_element_type=F32)


def dot_nn(left, right):
    return jnp.dot(left, right, preferred_element_type=F32)


def kernel(
    sizes,
    hidden_hbm,
    order_hbm,
    noisy_hbm,
    weight_hbm,
    mod_hbm,
    guidance_ref,
    index_ref,
    table_ref,
    mean_hbm,
    std_hbm,
    mix_hbm,
    mix_bias_hbm,
    conv_hbm,
    conv_bias_hbm,
    out_ref,
    x_buf,
    w_buf,
    rhs_buf,
    order_buf,
    noisy_buf,
    mod_buf,
    mean_buf,
    std_buf,
    mix_buf,
    mix_bias_buf,
    conv_buf,
    conv_bias_buf,
    lines_buf,
    latent_buf,
    taps_buf,
    cells_buf,
    partner_buf,
    center_buf,
    edge_buf,
    halo_buf,
    wide_buf,
    local_sem,
    chunk_sem,
    send_sem,
    recv_sem,
):
    seq_count, row_count, cfg_count, token_rows, token_cols, frames, chunks = sizes
    tokens = hidden_hbm.shape[1]
    width = hidden_hbm.shape[2]
    patch = weight_hbm.shape[0]
    chan = mix_hbm.shape[0]
    out_chan = conv_hbm.shape[2]
    slab_count = row_count * cfg_count
    step = width // chunks

    seq = lax.axis_index("seq")
    row = lax.axis_index("rows")
    half = lax.axis_index("cfg")
    slab = row * cfg_count + half

    small = []
    for source, target in (
        (mod_hbm, mod_buf),
        (order_hbm, order_buf),
        (noisy_hbm, noisy_buf),
        (mean_hbm, mean_buf),
        (std_hbm, std_buf),
        (mix_hbm, mix_buf),
        (mix_bias_hbm, mix_bias_buf),
        (conv_bias_hbm, conv_bias_buf),
        (conv_hbm, conv_buf),
    ):
        small.append(pltpu.make_async_copy(source, target, local_sem.at[len(small)]))
    loads = []
    weight_copy = pltpu.make_async_copy(weight_hbm, w_buf, chunk_sem.at[0])
    for part in range(chunks):
        columns = pl.ds(part * step, step)
        loads.append(
            pltpu.make_async_copy(
                hidden_hbm.at[0, :, columns],
                x_buf.at[:, columns],
                chunk_sem.at[1 + part],
            )
        )
    small[0].start()
    weight_copy.start()
    loads[0].start()
    for copy in small[1:-1]:
        copy.start()
    for copy in loads[1:]:
        copy.start()
    small[-1].start()

    barrier = pltpu.get_barrier_semaphore()

    def present(seq_step, slab_step):
        ok = jnp.bool_(True)
        if seq_step:
            ok = jnp.logical_and(ok, seq > 0 if seq_step < 0 else seq < seq_count - 1)
        if slab_step:
            ok = jnp.logical_and(ok, slab > 0 if slab_step < 0 else slab < slab_count - 1)
        return ok

    def place(seq_step, slab_step):
        other = slab + slab_step + cfg_count
        return {
            "seq": seq + seq_step,
            "rows": lax.div(other, cfg_count) - 1,
            "cfg": lax.rem(other, cfg_count),
        }

    around = [(a, b) for a in (-1, 0, 1) for b in (-1, 0, 1) if a or b]
    for offset in around:

        @pl.when(present(*offset))
        def _(offset=offset):
            pl.semaphore_signal(
                barrier, inc=1, device_id=place(*offset), device_id_type=pl.DeviceIdType.MESH
            )

    sends = ((0, 1), (0, -1), (1, 0), (1, 1), (1, -1))
    for slot, (seq_step, slab_step) in enumerate(sends):

        @pl.when(jnp.logical_not(present(-seq_step, -slab_step)))
        def _(slot=slot):
            if sends[slot][1]:
                halo_buf[slot] = jnp.zeros(halo_buf.shape[1:], BF16)
            else:
                center_buf[1] = jnp.zeros(center_buf.shape[1:], BF16)

    small[0].wait()
    scale = 1.0 + mod_buf[1:2, :]
    ones_row = lax.broadcasted_iota(jnp.int32, (EXTRA, width), 0) == 0
    rhs_buf[patch : patch + EXTRA, :] = jnp.where(ones_row, 1.0, 0.0).astype(BF16)

    for copy in small[1:-1]:
        copy.wait()
    cell = order_buf[...].astype(F32) + 0.5
    per_frame = float(row_count * token_rows * token_cols)
    frame_all = jnp.floor(cell * (1.0 / per_frame))
    in_frame = cell - frame_all * per_frame
    frame_pos = frame_all - frames * jnp.floor((frame_all + 0.5) * (1.0 / frames))
    row_all = jnp.floor(in_frame * (1.0 / token_cols))
    column = in_frame - 0.5 - row_all * token_cols
    row_pos = row_all - token_rows * jnp.floor((row_all + 0.5) * (1.0 / token_rows))
    target = (frame_pos * token_rows + row_pos) * token_cols + column
    wanted = lax.broadcasted_iota(jnp.int32, (tokens, tokens), 0).astype(F32)
    one_hot = jnp.where(jnp.abs(wanted - target) < 0.25, 1.0, 0.0).astype(BF16)
    weight_copy.wait()
    column_part = jnp.zeros((patch, LANES), F32)
    offset_part = jnp.zeros((patch, LANES), F32)
    for lane in range(0, width, LANES):
        lanes = slice(lane, lane + LANES)
        raw = w_buf[:, lanes].astype(F32)
        scaled = (raw * scale[:, lanes]).astype(BF16)
        rhs_buf[0:patch, lanes] = scaled
        column_part = column_part + scaled.astype(F32)
        offset_part = offset_part + raw * mod_buf[0:1, lanes]
    rest = jnp.concatenate([column_part, offset_part], axis=0)
    ones = jnp.ones((EXTRA, LANES), BF16)
    sums = jnp.zeros((EXTRA, 2 * patch), F32)
    for _ in range(3):
        piece = rest.astype(BF16)
        rest = rest - piece.astype(F32)
        sums = sums + dot_nt(ones, piece)
    column_sum = sums[0:1, 0:patch]
    offset_row = sums[0:1, patch:]

    block = 64
    blocks = tokens // block
    product = jnp.zeros((tokens, rhs_buf.shape[0]), F32)
    centers = [None] * blocks
    squares = [jnp.zeros((block, LANES), F32)] * blocks
    for part, hidden_copy in enumerate(loads):
        low = part * step
        hidden_copy.wait()
        product = product + dot_nt(x_buf[:, low : low + step], rhs_buf[:, low : low + step])
        for index in range(blocks):
            rows = slice(index * block, (index + 1) * block)
            if part == 0:
                total = x_buf[rows, 0:LANES].astype(F32)
                center = jnp.sum(total, axis=1, keepdims=True) * (1.0 / LANES)
                centers[index] = jnp.broadcast_to(center, (block, LANES))
            square = squares[index]
            for lane in range(low, low + step, LANES):
                gap = x_buf[rows, lane : lane + LANES].astype(F32) - centers[index]
                square = square + gap * gap
            squares[index] = square

    center = jnp.concatenate([value[:, 0:1] for value in centers], axis=0)
    spread = jnp.concatenate([jnp.sum(value, axis=1, keepdims=True) for value in squares], axis=0)
    average = product[:, patch : patch + 1] * (1.0 / width)
    spread = spread * (1.0 / width) - jnp.square(average - center)
    inverse = lax.rsqrt(spread + 1e-06)
    head = (product[:, 0:patch] - average * column_sum) * inverse + offset_row

    head_high, head_low = split_bf16(head)
    placed = dot_nn(one_hot, jnp.concatenate([head_high, head_low], axis=1))
    placed = placed[:, 0:patch] + placed[:, patch:]
    per = token_rows * token_cols
    for index in range(token_rows):
        pieces = [
            placed[f * per + index * token_cols : f * per + (index + 1) * token_cols, :]
            for f in range(frames)
        ]
        cells_buf[index] = jnp.concatenate(pieces, axis=1)

    slab_peers = (slab > 0).astype(jnp.int32) + (slab < slab_count - 1).astype(jnp.int32)
    seq_peers = (seq > 0).astype(jnp.int32) + (seq < seq_count - 1).astype(jnp.int32)
    pl.semaphore_wait(barrier, (1 + slab_peers) * (1 + seq_peers) - 1)

    pair = pltpu.make_async_remote_copy(
        src_ref=cells_buf.at[1 - half],
        dst_ref=partner_buf,
        send_sem=send_sem.at[0],
        recv_sem=recv_sem.at[0],
        device_id={"cfg": 1 - half},
        device_id_type=pl.DeviceIdType.MESH,
    )
    pair.start()

    for f in range(frames):
        for a in range(2):
            for g in range(lines_buf.shape[2]):
                lines_buf[f, a, g : g + 1, :] = noisy_buf[f, a : a + 1, g * LANES : (g + 1) * LANES]
    lane = lax.broadcasted_iota(jnp.int32, (lines_buf.shape[2], LANES), 1)
    span = 2 * chan
    per_line = LANES // span
    groups = lines_buf.shape[2]
    for jj in range(per_line):
        line = jnp.zeros((groups, LANES), F32)
        for f in range(frames):
            for a in range(2):
                slot = f * 2 + a
                moved = lines_buf[f, a]
                if (slot - jj) % per_line:
                    moved = pltpu.roll(moved, ((slot - jj) * span) % LANES, 1)
                line = jnp.where((lane >= slot * span) & (lane < (slot + 1) * span), moved, line)
        latent_buf[pl.ds(jj, groups, stride=per_line), :] = line

    repeat = LANES // chan

    def lanes_of(ref):
        return jnp.concatenate([ref[...]] * repeat, axis=1)

    mean_row = lanes_of(mean_buf)
    std_row = lanes_of(std_buf)
    mix_row = lanes_of(mix_bias_buf)
    mix = jnp.concatenate([lanes_of(mix_buf)] * repeat, axis=0)
    mix_in = lax.broadcasted_iota(jnp.int32, (LANES, LANES), 0)
    mix_out = lax.broadcasted_iota(jnp.int32, (LANES, LANES), 1)
    group_in = lax.div(mix_in, chan)
    wanted_out = (
        lax.rem(lax.div(group_in, 2), 2) * (2 * frames)
        + lax.div(group_in, 4) * 2
        + lax.rem(group_in, 2)
    )
    same = wanted_out == lax.div(mix_out, chan)
    mix_high, mix_low = split_bf16(jnp.where(same, mix, 0.0))
    mix_both = jnp.concatenate([mix_high, mix_low], axis=1)

    at = index_ref[0]
    now = jnp.full((1, LANES), table_ref[at].astype(F32))
    later = jnp.full((1, LANES), table_ref[at + 1].astype(F32))
    step_size = later / 1000.0 - now / 1000.0

    pair.wait_recv()
    own = cells_buf[half]
    partner = partner_buf[...]
    cond = jnp.where(half == 0, own, partner)
    free = jnp.where(half == 0, partner, own)
    velocity = free + guidance_ref[0] * (cond - free)
    stepped = latent_buf[...] + step_size * velocity
    channels = stepped * std_row + mean_row
    high, low = split_bf16(channels)
    mixed = dot_nn(jnp.concatenate([high, low], axis=0), mix_both)
    mixed = mixed[0:token_cols, 0:LANES] + (
        mixed[0:token_cols, LANES:] + mixed[token_cols:, 0:LANES]
    )
    latent = (mixed + mix_row).astype(BF16)
    exact = latent.astype(F32)
    fold = token_cols // 2
    left = lax.broadcasted_iota(jnp.int32, (fold, LANES), 1) < LANES // 2
    first, second = exact[0:fold], exact[fold:]
    edge_buf[0] = jnp.where(left, first, pltpu.roll(second, LANES // 2, 1)).astype(BF16)
    edge_buf[1] = jnp.where(left, pltpu.roll(first, LANES // 2, 1), second).astype(BF16)
    center_buf[0] = latent

    copies = []
    for slot, (seq_step, slab_step) in enumerate(sends):
        if slab_step:
            source, target = edge_buf.at[(1 + slab_step) // 2], halo_buf.at[slot]
        else:
            source, target = center_buf.at[0], center_buf.at[1]
        copy = pltpu.make_async_remote_copy(
            src_ref=source,
            dst_ref=target,
            send_sem=send_sem.at[1 + slot],
            recv_sem=recv_sem.at[1 + slot],
            device_id=place(seq_step, slab_step),
            device_id_type=pl.DeviceIdType.MESH,
        )
        copies.append(copy)
    for slot in (3, 4, 2, 0, 1):
        pl.when(present(*sends[slot]))(copies[slot].start)

    small[-1].wait()
    position = 0
    for t in range(3):
        for shifted in range(2):
            for u in range(4):
                for e_in in range(2):
                    dx = (2 - 3 * e_in) if shifted else e_in
                    for e_out in range(2):
                        w = dx - e_out + 1
                        columns = slice(e_out * out_chan, (e_out + 1) * out_chan)
                        if u < 3 and 0 <= w <= 2:
                            value = conv_buf[(t * 3 + u) * 3 + w]
                        else:
                            value = jnp.zeros((chan, out_chan), BF16)
                        taps_buf[position : position + chan, columns] = value
                    position += chan

    lane = lax.broadcasted_iota(jnp.int32, (token_cols, LANES), 1)
    line = lax.broadcasted_iota(jnp.int32, (token_cols, LANES), 0)
    odd = lax.rem(lax.div(lane, chan), 2) == 1

    def turned(value, amount):
        return pltpu.roll(value, amount % LANES, 1) if amount % LANES else value

    def spread_rows(block, f, lane_base):
        return jnp.concatenate(
            [turned(block, lane_base - (part * frames + f) * span) for part in range(2)], axis=0
        )

    def middle_rows(block, f):
        return jnp.where(
            lane >= 2 * span, turned(block, -f * span), turned(block, span - f * span)
        )

    def tap_rows(full, above, below, f):
        full = jnp.where(lane < span, spread_rows(above, f, 0), full)
        full = jnp.where(lane >= 3 * span, spread_rows(below, f, 3 * span), full)
        before = jnp.where(line == 0, 0.0, pltpu.roll(full, 1, 0))
        after = jnp.where(line == token_cols - 1, 0.0, pltpu.roll(full, token_cols - 1, 0))
        beside = jnp.where(odd, before, after)
        upper = jnp.concatenate([full, beside], axis=1)
        lower = jnp.concatenate([turned(full, -span), turned(beside, -span)], axis=1)
        return jnp.concatenate([upper, lower], axis=0).astype(BF16)

    def arrived(slot):
        seq_step, slab_step = sends[slot]
        pl.when(present(-seq_step, -slab_step))(copies[slot].wait_recv)

    own_middle = [middle_rows(exact, f) for f in range(frames)]
    depth = 2 * LANES
    for slot in (2, 3, 4):
        arrived(slot)
    center_block = center_buf[1].astype(F32)
    above, below = halo_buf[3].astype(F32), halo_buf[4].astype(F32)
    earlier = [
        tap_rows(middle_rows(center_block, f), above, below, f) for f in range(frames)
    ]
    partial = []
    for f in range(frames):
        count = min(2, frames - f)
        partial.append(
            dot_nn(
                jnp.concatenate(earlier[f : f + count], axis=1), taps_buf[0 : count * depth, :]
            )
        )
    for slot in (0, 1):
        arrived(slot)
    above, below = halo_buf[0].astype(F32), halo_buf[1].astype(F32)
    current = [tap_rows(own_middle[f], above, below, f) for f in range(frames)]
    bias = conv_bias_buf[...]
    for f in range(frames):
        count = min(2, frames - f)
        result = partial[f] + dot_nn(
            jnp.concatenate(current[f + count - frames : f + 1], axis=1),
            taps_buf[count * depth :, :],
        )
        for y in range(2):
            first = (f * 2 + y) * token_cols
            for part in range(out_chan // LANES):
                lanes = slice(part * LANES, (part + 1) * LANES)
                for e in range(2):
                    from_lane = e * out_chan + part * LANES
                    wide_buf[part, pl.ds(2 * first + e, token_cols, stride=2), :] = (
                        result[y * token_cols : (y + 1) * token_cols, from_lane : from_lane + LANES]
                        + bias[part : part + 1, :]
                    )
                out_ref[f, y, :, lanes] = wide_buf[
                    part, 2 * first : 2 * first + 2 * token_cols, :
                ].astype(BF16)

    pair.wait_send()
    for slot in range(len(sends)):
        pl.when(present(*sends[slot]))(copies[slot].wait_send)


def per_device(
    counts,
    hidden,
    token_order,
    noisy_latent,
    head_weight,
    head_mod,
    guidance,
    timestep_index,
    step_table,
    vae_mean,
    vae_std,
    conv2_weight,
    conv2_bias,
    conv1_weight,
    conv1_bias,
):
    frames, lat_rows, lat_width = noisy_latent.shape
    chan = vae_mean.shape[0]
    tokens, width = hidden.shape[1:]
    patch = head_weight.shape[1]
    out_chan = conv1_weight.shape[2]
    token_cols = lat_width // (2 * chan)
    token_rows = lat_rows * counts[2] // 2
    chunks = 5
    operands = (
        hidden,
        token_order.reshape(1, -1),
        noisy_latent,
        head_weight.T,
        head_mod,
        guidance,
        timestep_index,
        step_table,
        vae_mean.reshape(1, -1),
        vae_std.reshape(1, -1),
        conv2_weight,
        conv2_bias.reshape(1, -1),
        conv1_weight,
        conv1_bias.reshape(-1, LANES),
    )
    block = (token_cols, LANES)
    scratch = [
        pltpu.VMEM((tokens, width), BF16),
        pltpu.VMEM((patch, width), BF16),
        pltpu.VMEM((patch + EXTRA, width), BF16),
        pltpu.VMEM(operands[1].shape, jnp.int32),
        pltpu.VMEM(operands[2].shape, F32),
    ]
    scratch += [
        pltpu.VMEM(value.shape, value.dtype)
        for index, value in enumerate(operands)
        if index == 4 or index > 7
    ]
    scratch += [
        pltpu.VMEM((frames, lat_rows, lat_width // LANES, LANES), F32),
        pltpu.VMEM(block, F32),
        pltpu.VMEM((3 * 16 * chan, 2 * out_chan), BF16),
        pltpu.VMEM((token_rows,) + block, F32),
        pltpu.VMEM(block, F32),
        pltpu.VMEM((2,) + block, BF16),
        pltpu.VMEM((2, token_cols // 2, LANES), BF16),
        pltpu.VMEM((5, token_cols // 2, LANES), BF16),
        pltpu.VMEM((out_chan // LANES, frames * lat_rows * 2 * token_cols, LANES), F32),
        pltpu.SemaphoreType.DMA((9,)),
        pltpu.SemaphoreType.DMA((1 + chunks,)),
        pltpu.SemaphoreType.DMA((6,)),
        pltpu.SemaphoreType.DMA((6,)),
    ]
    sizes = tuple(counts) + (token_rows, token_cols, frames, chunks)
    return pl.pallas_call(
        functools.partial(kernel, sizes),
        out_shape=pltpu.VMEM((frames, lat_rows, 2 * token_cols, out_chan), BF16),
        in_specs=[
            pl.BlockSpec(memory_space=pltpu.SMEM if index in (5, 6, 7) else pl.ANY)
            for index in range(len(operands))
        ],
        out_specs=pl.BlockSpec(memory_space=pltpu.VMEM),
        scratch_shapes=scratch,
        compiler_params=pltpu.CompilerParams(
            collective_id=0, has_side_effects=True, vmem_limit_bytes=60 * 1024 * 1024
        ),
        name="guided_step",
    )(
        *[
            value
            if index in (5, 6, 7)
            else pltpu.with_memory_space_constraint(value, pltpu.HBM)
            for index, value in enumerate(operands)
        ]
    )


def solution(mesh):
    counts = (mesh.shape["seq"], mesh.shape["rows"], mesh.shape["cfg"])
    return jax.shard_map(
        functools.partial(per_device, counts),
        mesh=mesh,
        in_specs=(
            P("cfg", ("groups", "seq", "rows"), None),
            P(("groups", "seq", "rows")),
            P(("groups", "seq"), ("rows", "cfg"), None),
            P(),
            P(),
            P(),
            P(),
            P(),
            P(),
            P(),
            P(),
            P(),
            P(),
            P(),
        ),
        out_specs=P(("groups", "seq"), ("rows", "cfg"), None, None),
        check_vma=False,
    )
```

```python
import functools

import jax
import jax.numpy as jnp
from jax import lax
from jax.experimental import pallas as pl
from jax.experimental.pallas import tpu as pltpu
from jax.sharding import PartitionSpec as P

F32 = jnp.float32
BF16 = jnp.bfloat16
LANES = 128
EXTRA = 16


def split_bf16(value):
    high = value.astype(BF16)
    low = (value - high.astype(F32)).astype(BF16)
    return high, low


def dot_nt(left, right):
    return lax.dot_general(left, right, (((1,), (1,)), ((), ())), preferred_element_type=F32)


def dot_nn(left, right):
    return jnp.dot(left, right, preferred_element_type=F32)


def kernel(
    sizes,
    hidden_hbm,
    order_hbm,
    noisy_hbm,
    weight_hbm,
    mod_hbm,
    guidance_ref,
    index_ref,
    table_ref,
    mean_hbm,
    std_hbm,
    mix_hbm,
    mix_bias_hbm,
    conv_hbm,
    conv_bias_hbm,
    out_ref,
    x_buf,
    w_buf,
    rhs_buf,
    order_buf,
    noisy_buf,
    mod_buf,
    mean_buf,
    std_buf,
    mix_buf,
    mix_bias_buf,
    conv_buf,
    conv_bias_buf,
    lines_buf,
    latent_buf,
    taps_buf,
    cells_buf,
    partner_buf,
    center_buf,
    edge_buf,
    halo_buf,
    wide_buf,
    local_sem,
    chunk_sem,
    send_sem,
    recv_sem,
):
    seq_count, row_count, cfg_count, token_rows, token_cols, frames, chunks = sizes
    tokens = hidden_hbm.shape[1]
    width = hidden_hbm.shape[2]
    patch = weight_hbm.shape[0]
    chan = mix_hbm.shape[0]
    out_chan = conv_hbm.shape[2]
    slab_count = row_count * cfg_count
    step = width // chunks

    seq = lax.axis_index("seq")
    row = lax.axis_index("rows")
    half = lax.axis_index("cfg")
    slab = row * cfg_count + half

    small = []
    for source, target in (
        (mod_hbm, mod_buf),
        (order_hbm, order_buf),
        (noisy_hbm, noisy_buf),
        (mean_hbm, mean_buf),
        (std_hbm, std_buf),
        (mix_hbm, mix_buf),
        (mix_bias_hbm, mix_bias_buf),
        (conv_bias_hbm, conv_bias_buf),
        (conv_hbm, conv_buf),
    ):
        small.append(pltpu.make_async_copy(source, target, local_sem.at[len(small)]))
    loads = []
    weight_copy = pltpu.make_async_copy(weight_hbm, w_buf, chunk_sem.at[0])
    for part in range(chunks):
        columns = pl.ds(part * step, step)
        loads.append(
            pltpu.make_async_copy(
                hidden_hbm.at[0, :, columns],
                x_buf.at[pl.ds(0, tokens), columns],
                chunk_sem.at[1 + part],
            )
        )
    small[0].start()
    weight_copy.start()
    loads[0].start()
    for copy in small[1:-1]:
        copy.start()
    for copy in loads[1:]:
        copy.start()
    small[-1].start()

    barrier = pltpu.get_barrier_semaphore()

    def present(seq_step, slab_step):
        ok = jnp.bool_(True)
        if seq_step:
            ok = jnp.logical_and(ok, seq > 0 if seq_step < 0 else seq < seq_count - 1)
        if slab_step:
            ok = jnp.logical_and(ok, slab > 0 if slab_step < 0 else slab < slab_count - 1)
        return ok

    def place(seq_step, slab_step):
        other = slab + slab_step + cfg_count
        return {
            "seq": seq + seq_step,
            "rows": lax.div(other, cfg_count) - 1,
            "cfg": lax.rem(other, cfg_count),
        }

    around = [(a, b) for a in (-1, 0, 1) for b in (-1, 0, 1) if a or b]
    for offset in around:

        @pl.when(present(*offset))
        def _(offset=offset):
            pl.semaphore_signal(
                barrier, inc=1, device_id=place(*offset), device_id_type=pl.DeviceIdType.MESH
            )

    sends = ((0, 1), (0, -1), (1, 0), (1, 1), (1, -1))
    for slot, (seq_step, slab_step) in enumerate(sends):

        @pl.when(jnp.logical_not(present(-seq_step, -slab_step)))
        def _(slot=slot):
            if sends[slot][1]:
                halo_buf[slot] = jnp.zeros(halo_buf.shape[1:], BF16)
            else:
                center_buf[1] = jnp.zeros(center_buf.shape[1:], BF16)

    small[0].wait()
    scale = 1.0 + mod_buf[1:2, :]
    shift_high, shift_low = split_bf16(mod_buf[0:1, :])
    pick = lax.broadcasted_iota(jnp.int32, (EXTRA, width), 0)
    x_buf[tokens : tokens + EXTRA, :] = jnp.where(
        pick == 0,
        shift_high.astype(F32),
        jnp.where(pick == 1, shift_low.astype(F32), jnp.where(pick == 2, 1.0, 0.0)),
    ).astype(BF16)
    ones_row = lax.broadcasted_iota(jnp.int32, (EXTRA, width), 0) == 0
    rhs_buf[2 * patch : 2 * patch + EXTRA, :] = jnp.where(ones_row, 1.0, 0.0).astype(BF16)

    for copy in small[1:-1]:
        copy.wait()
    cell = order_buf[...].astype(F32) + 0.5
    per_frame = float(row_count * token_rows * token_cols)
    frame_all = jnp.floor(cell * (1.0 / per_frame))
    in_frame = cell - frame_all * per_frame
    frame_pos = frame_all - frames * jnp.floor((frame_all + 0.5) * (1.0 / frames))
    row_all = jnp.floor(in_frame * (1.0 / token_cols))
    column = in_frame - 0.5 - row_all * token_cols
    row_pos = row_all - token_rows * jnp.floor((row_all + 0.5) * (1.0 / token_rows))
    target = (frame_pos * token_rows + row_pos) * token_cols + column
    wanted = lax.broadcasted_iota(jnp.int32, (tokens, tokens), 0).astype(F32)
    one_hot = jnp.where(jnp.abs(wanted - target) < 0.25, 1.0, 0.0).astype(BF16)
    for f in range(frames):
        for a in range(2):
            for g in range(lines_buf.shape[2]):
                lines_buf[f, a, g : g + 1, :] = noisy_buf[f, a : a + 1, g * LANES : (g + 1) * LANES]
    lane = lax.broadcasted_iota(jnp.int32, (lines_buf.shape[2], LANES), 1)
    span = 2 * chan
    per_line = LANES // span
    groups = lines_buf.shape[2]
    for jj in range(per_line):
        line = jnp.zeros((groups, LANES), F32)
        for f in range(frames):
            for a in range(2):
                slot = f * 2 + a
                moved = lines_buf[f, a]
                if (slot - jj) % per_line:
                    moved = pltpu.roll(moved, ((slot - jj) * span) % LANES, 1)
                line = jnp.where((lane >= slot * span) & (lane < (slot + 1) * span), moved, line)
        latent_buf[pl.ds(jj, groups, stride=per_line), :] = line

    repeat = LANES // chan

    def lanes_of(ref):
        return jnp.concatenate([ref[...]] * repeat, axis=1)

    mean_row = lanes_of(mean_buf)
    std_row = lanes_of(std_buf)
    mix_row = lanes_of(mix_bias_buf)
    mix = jnp.concatenate([lanes_of(mix_buf)] * repeat, axis=0)
    mix_in = lax.broadcasted_iota(jnp.int32, (LANES, LANES), 0)
    mix_out = lax.broadcasted_iota(jnp.int32, (LANES, LANES), 1)
    group_in = lax.div(mix_in, chan)
    wanted_out = (
        lax.rem(lax.div(group_in, 2), 2) * (2 * frames)
        + lax.div(group_in, 4) * 2
        + lax.rem(group_in, 2)
    )
    same = wanted_out == lax.div(mix_out, chan)
    mix_high, mix_low = split_bf16(jnp.where(same, mix, 0.0))
    mix_both = jnp.concatenate([mix_high, mix_low], axis=1)

    at = index_ref[0]
    now = jnp.full((1, LANES), table_ref[at].astype(F32))
    later = jnp.full((1, LANES), table_ref[at + 1].astype(F32))
    step_size = later / 1000.0 - now / 1000.0

    weight_copy.wait()
    rhs_buf[0:patch, :] = (w_buf[...].astype(F32) * scale).astype(BF16)
    rhs_buf[patch : 2 * patch, :] = w_buf[...]

    block = 64
    blocks = tokens // block
    product = jnp.zeros((tokens + EXTRA, rhs_buf.shape[0]), F32)
    centers = [None] * blocks
    squares = [jnp.zeros((block, LANES), F32)] * blocks
    for part, hidden_copy in enumerate(loads):
        low = part * step
        hidden_copy.wait()
        product = product + dot_nt(x_buf[:, low : low + step], rhs_buf[:, low : low + step])
        for index in range(blocks):
            rows = slice(index * block, (index + 1) * block)
            if part == 0:
                total = x_buf[rows, 0:LANES].astype(F32)
                center = jnp.sum(total, axis=1, keepdims=True) * (1.0 / LANES)
                centers[index] = jnp.broadcast_to(center, (block, LANES))
            square = squares[index]
            for lane in range(low, low + step, LANES):
                gap = x_buf[rows, lane : lane + LANES].astype(F32) - centers[index]
                square = square + gap * gap
            squares[index] = square

    center = jnp.concatenate([value[:, 0:1] for value in centers], axis=0)
    spread = jnp.concatenate([jnp.sum(value, axis=1, keepdims=True) for value in squares], axis=0)
    average = product[0:tokens, 2 * patch : 2 * patch + 1] * (1.0 / width)
    spread = spread * (1.0 / width) - jnp.square(average - center)
    inverse = lax.rsqrt(spread + 1e-06)
    column_sum = product[tokens + 2 : tokens + 3, 0:patch]
    both = product[tokens : tokens + 1, :] + product[tokens + 1 : tokens + 2, :]
    offset_row = both[:, patch : 2 * patch]
    head = (product[0:tokens, 0:patch] - average * column_sum) * inverse + offset_row

    head_high, head_low = split_bf16(head)
    placed = dot_nn(one_hot, jnp.concatenate([head_high, head_low], axis=1))
    placed = placed[:, 0:patch] + placed[:, patch:]
    per = token_rows * token_cols
    for index in range(token_rows):
        pieces = [
            placed[f * per + index * token_cols : f * per + (index + 1) * token_cols, :]
            for f in range(frames)
        ]
        cells_buf[index] = jnp.concatenate(pieces, axis=1)

    slab_peers = (slab > 0).astype(jnp.int32) + (slab < slab_count - 1).astype(jnp.int32)
    seq_peers = (seq > 0).astype(jnp.int32) + (seq < seq_count - 1).astype(jnp.int32)
    pl.semaphore_wait(barrier, (1 + slab_peers) * (1 + seq_peers) - 1)

    pair = pltpu.make_async_remote_copy(
        src_ref=cells_buf.at[1 - half],
        dst_ref=partner_buf,
        send_sem=send_sem.at[0],
        recv_sem=recv_sem.at[0],
        device_id={"cfg": 1 - half},
        device_id_type=pl.DeviceIdType.MESH,
    )
    pair.start()

    pair.wait_recv()
    own = cells_buf[half]
    partner = partner_buf[...]
    cond = jnp.where(half == 0, own, partner)
    free = jnp.where(half == 0, partner, own)
    velocity = free + guidance_ref[0] * (cond - free)
    stepped = latent_buf[...] + step_size * velocity
    channels = stepped * std_row + mean_row
    high, low = split_bf16(channels)
    mixed = dot_nn(jnp.concatenate([high, low], axis=0), mix_both)
    mixed = mixed[0:token_cols, 0:LANES] + (
        mixed[0:token_cols, LANES:] + mixed[token_cols:, 0:LANES]
    )
    latent = (mixed + mix_row).astype(BF16)
    exact = latent.astype(F32)
    fold = token_cols // 2
    left = lax.broadcasted_iota(jnp.int32, (fold, LANES), 1) < LANES // 2
    first, second = exact[0:fold], exact[fold:]
    edge_buf[0] = jnp.where(left, first, pltpu.roll(second, LANES // 2, 1)).astype(BF16)
    edge_buf[1] = jnp.where(left, pltpu.roll(first, LANES // 2, 1), second).astype(BF16)
    center_buf[0] = latent

    copies = []
    for slot, (seq_step, slab_step) in enumerate(sends):
        if slab_step:
            source, target = edge_buf.at[(1 + slab_step) // 2], halo_buf.at[slot]
        else:
            source, target = center_buf.at[0], center_buf.at[1]
        copy = pltpu.make_async_remote_copy(
            src_ref=source,
            dst_ref=target,
            send_sem=send_sem.at[1 + slot],
            recv_sem=recv_sem.at[1 + slot],
            device_id=place(seq_step, slab_step),
            device_id_type=pl.DeviceIdType.MESH,
        )
        copies.append(copy)
    for slot in (3, 4, 2, 0, 1):
        pl.when(present(*sends[slot]))(copies[slot].start)

    small[-1].wait()
    position = 0
    for t in range(3):
        for shifted in range(2):
            for u in range(4):
                for e_in in range(2):
                    dx = (2 - 3 * e_in) if shifted else e_in
                    for e_out in range(2):
                        w = dx - e_out + 1
                        columns = slice(e_out * out_chan, (e_out + 1) * out_chan)
                        if u < 3 and 0 <= w <= 2:
                            value = conv_buf[(t * 3 + u) * 3 + w]
                        else:
                            value = jnp.zeros((chan, out_chan), BF16)
                        taps_buf[position : position + chan, columns] = value
                    position += chan

    lane = lax.broadcasted_iota(jnp.int32, (token_cols, LANES), 1)
    line = lax.broadcasted_iota(jnp.int32, (token_cols, LANES), 0)
    odd = lax.rem(lax.div(lane, chan), 2) == 1

    def turned(value, amount):
        return pltpu.roll(value, amount % LANES, 1) if amount % LANES else value

    def spread_rows(block, f, lane_base):
        return jnp.concatenate(
            [turned(block, lane_base - (part * frames + f) * span) for part in range(2)], axis=0
        )

    def middle_rows(block, f):
        return jnp.where(
            lane >= 2 * span, turned(block, -f * span), turned(block, span - f * span)
        )

    def tap_rows(full, above, below, f):
        full = jnp.where(lane < span, spread_rows(above, f, 0), full)
        full = jnp.where(lane >= 3 * span, spread_rows(below, f, 3 * span), full)
        before = jnp.where(line == 0, 0.0, pltpu.roll(full, 1, 0))
        after = jnp.where(line == token_cols - 1, 0.0, pltpu.roll(full, token_cols - 1, 0))
        beside = jnp.where(odd, before, after)
        upper = jnp.concatenate([full, beside], axis=1)
        lower = jnp.concatenate([turned(full, -span), turned(beside, -span)], axis=1)
        return jnp.concatenate([upper, lower], axis=0).astype(BF16)

    def arrived(slot):
        seq_step, slab_step = sends[slot]
        pl.when(present(-seq_step, -slab_step))(copies[slot].wait_recv)

    own_middle = [middle_rows(exact, f) for f in range(frames)]
    depth = 2 * LANES
    for slot in (2, 3, 4):
        arrived(slot)
    center_block = center_buf[1].astype(F32)
    above, below = halo_buf[3].astype(F32), halo_buf[4].astype(F32)
    earlier = [
        tap_rows(middle_rows(center_block, f), above, below, f) for f in range(frames)
    ]
    partial = []
    for f in range(frames):
        count = min(2, frames - f)
        partial.append(
            dot_nn(
                jnp.concatenate(earlier[f : f + count], axis=1), taps_buf[0 : count * depth, :]
            )
        )
    for slot in (0, 1):
        arrived(slot)
    above, below = halo_buf[0].astype(F32), halo_buf[1].astype(F32)
    current = [tap_rows(own_middle[f], above, below, f) for f in range(frames)]
    bias = conv_bias_buf[...]
    for f in range(frames):
        count = min(2, frames - f)
        result = partial[f] + dot_nn(
            jnp.concatenate(current[f + count - frames : f + 1], axis=1),
            taps_buf[count * depth :, :],
        )
        for y in range(2):
            first = (f * 2 + y) * token_cols
            for part in range(out_chan // LANES):
                lanes = slice(part * LANES, (part + 1) * LANES)
                for e in range(2):
                    from_lane = e * out_chan + part * LANES
                    wide_buf[part, pl.ds(2 * first + e, token_cols, stride=2), :] = (
                        result[y * token_cols : (y + 1) * token_cols, from_lane : from_lane + LANES]
                        + bias[part : part + 1, :]
                    )
                out_ref[f, y, :, lanes] = wide_buf[
                    part, 2 * first : 2 * first + 2 * token_cols, :
                ].astype(BF16)

    pair.wait_send()
    for slot in range(len(sends)):
        pl.when(present(*sends[slot]))(copies[slot].wait_send)


def per_device(
    counts,
    hidden,
    token_order,
    noisy_latent,
    head_weight,
    head_mod,
    guidance,
    timestep_index,
    step_table,
    vae_mean,
    vae_std,
    conv2_weight,
    conv2_bias,
    conv1_weight,
    conv1_bias,
):
    frames, lat_rows, lat_width = noisy_latent.shape
    chan = vae_mean.shape[0]
    tokens, width = hidden.shape[1:]
    patch = head_weight.shape[1]
    out_chan = conv1_weight.shape[2]
    token_cols = lat_width // (2 * chan)
    token_rows = lat_rows * counts[2] // 2
    chunks = 5
    operands = (
        hidden,
        token_order.reshape(1, -1),
        noisy_latent,
        head_weight.T,
        head_mod,
        guidance,
        timestep_index,
        step_table,
        vae_mean.reshape(1, -1),
        vae_std.reshape(1, -1),
        conv2_weight,
        conv2_bias.reshape(1, -1),
        conv1_weight,
        conv1_bias.reshape(-1, LANES),
    )
    block = (token_cols, LANES)
    scratch = [
        pltpu.VMEM((tokens + EXTRA, width), BF16),
        pltpu.VMEM((patch, width), BF16),
        pltpu.VMEM((2 * patch + EXTRA, width), BF16),
        pltpu.VMEM(operands[1].shape, jnp.int32),
        pltpu.VMEM(operands[2].shape, F32),
    ]
    scratch += [
        pltpu.VMEM(value.shape, value.dtype)
        for index, value in enumerate(operands)
        if index == 4 or index > 7
    ]
    scratch += [
        pltpu.VMEM((frames, lat_rows, lat_width // LANES, LANES), F32),
        pltpu.VMEM(block, F32),
        pltpu.VMEM((3 * 16 * chan, 2 * out_chan), BF16),
        pltpu.VMEM((token_rows,) + block, F32),
        pltpu.VMEM(block, F32),
        pltpu.VMEM((2,) + block, BF16),
        pltpu.VMEM((2, token_cols // 2, LANES), BF16),
        pltpu.VMEM((5, token_cols // 2, LANES), BF16),
        pltpu.VMEM((out_chan // LANES, frames * lat_rows * 2 * token_cols, LANES), F32),
        pltpu.SemaphoreType.DMA((9,)),
        pltpu.SemaphoreType.DMA((1 + chunks,)),
        pltpu.SemaphoreType.DMA((6,)),
        pltpu.SemaphoreType.DMA((6,)),
    ]
    sizes = tuple(counts) + (token_rows, token_cols, frames, chunks)
    return pl.pallas_call(
        functools.partial(kernel, sizes),
        out_shape=pltpu.VMEM((frames, lat_rows, 2 * token_cols, out_chan), BF16),
        in_specs=[
            pl.BlockSpec(memory_space=pltpu.SMEM if index in (5, 6, 7) else pl.ANY)
            for index in range(len(operands))
        ],
        out_specs=pl.BlockSpec(memory_space=pltpu.VMEM),
        scratch_shapes=scratch,
        compiler_params=pltpu.CompilerParams(
            collective_id=0, has_side_effects=True, vmem_limit_bytes=60 * 1024 * 1024
        ),
        name="guided_step",
    )(
        *[
            value
            if index in (5, 6, 7)
            else pltpu.with_memory_space_constraint(value, pltpu.HBM)
            for index, value in enumerate(operands)
        ]
    )


def solution(mesh):
    counts = (mesh.shape["seq"], mesh.shape["rows"], mesh.shape["cfg"])
    return jax.shard_map(
        functools.partial(per_device, counts),
        mesh=mesh,
        in_specs=(
            P("cfg", ("groups", "seq", "rows"), None),
            P(("groups", "seq", "rows")),
            P(("groups", "seq"), ("rows", "cfg"), None),
            P(),
            P(),
            P(),
            P(),
            P(),
            P(),
            P(),
            P(),
            P(),
            P(),
            P(),
        ),
        out_specs=P(("groups", "seq"), ("rows", "cfg"), None, None),
        check_vma=False,
    )
```

```python
import functools

import jax
import jax.numpy as jnp
from jax import lax
from jax.experimental import pallas as pl
from jax.experimental.pallas import tpu as pltpu
from jax.sharding import PartitionSpec as P

F32 = jnp.float32
BF16 = jnp.bfloat16
LANES = 128
EXTRA = 16


def split_bf16(value):
    high = value.astype(BF16)
    low = (value - high.astype(F32)).astype(BF16)
    return high, low


def dot_nt(left, right):
    return lax.dot_general(left, right, (((1,), (1,)), ((), ())), preferred_element_type=F32)


def dot_nn(left, right):
    return jnp.dot(left, right, preferred_element_type=F32)


def kernel(
    sizes,
    hidden_hbm,
    order_hbm,
    noisy_hbm,
    weight_hbm,
    mod_hbm,
    guidance_ref,
    index_ref,
    table_ref,
    mean_hbm,
    std_hbm,
    mix_hbm,
    mix_bias_hbm,
    conv_hbm,
    conv_bias_hbm,
    out_ref,
    x_buf,
    w_buf,
    rhs_buf,
    order_buf,
    noisy_buf,
    mod_buf,
    mean_buf,
    std_buf,
    mix_buf,
    mix_bias_buf,
    conv_buf,
    conv_bias_buf,
    lines_buf,
    latent_buf,
    taps_buf,
    cells_buf,
    partner_buf,
    center_buf,
    edge_buf,
    halo_buf,
    wide_buf,
    local_sem,
    chunk_sem,
    send_sem,
    recv_sem,
):
    seq_count, row_count, cfg_count, token_rows, token_cols, frames, chunks = sizes
    tokens = hidden_hbm.shape[1]
    width = hidden_hbm.shape[2]
    patch = weight_hbm.shape[0]
    chan = mix_hbm.shape[0]
    out_chan = conv_hbm.shape[2]
    slab_count = row_count * cfg_count
    step = width // chunks

    seq = lax.axis_index("seq")
    row = lax.axis_index("rows")
    half = lax.axis_index("cfg")
    slab = row * cfg_count + half

    small = []
    for source, target in (
        (mod_hbm, mod_buf),
        (order_hbm, order_buf),
        (noisy_hbm, noisy_buf),
        (mean_hbm, mean_buf),
        (std_hbm, std_buf),
        (mix_hbm, mix_buf),
        (mix_bias_hbm, mix_bias_buf),
        (conv_bias_hbm, conv_bias_buf),
        (conv_hbm, conv_buf),
    ):
        small.append(pltpu.make_async_copy(source, target, local_sem.at[len(small)]))
    loads = []
    weight_copy = pltpu.make_async_copy(weight_hbm, w_buf, chunk_sem.at[0])
    for part in range(chunks):
        columns = pl.ds(part * step, step)
        loads.append(
            pltpu.make_async_copy(
                hidden_hbm.at[0, :, columns],
                x_buf.at[pl.ds(0, tokens), columns],
                chunk_sem.at[1 + part],
            )
        )
    for copy in small[:-1]:
        copy.start()
    weight_copy.start()
    for copy in loads:
        copy.start()
    small[-1].start()

    barrier = pltpu.get_barrier_semaphore()

    def present(seq_step, slab_step):
        ok = jnp.bool_(True)
        if seq_step:
            ok = jnp.logical_and(ok, seq > 0 if seq_step < 0 else seq < seq_count - 1)
        if slab_step:
            ok = jnp.logical_and(ok, slab > 0 if slab_step < 0 else slab < slab_count - 1)
        return ok

    def place(seq_step, slab_step):
        other = slab + slab_step + cfg_count
        return {
            "seq": seq + seq_step,
            "rows": lax.div(other, cfg_count) - 1,
            "cfg": lax.rem(other, cfg_count),
        }

    around = [(a, b) for a in (-1, 0, 1) for b in (-1, 0, 1) if a or b]
    for offset in around:

        @pl.when(present(*offset))
        def _(offset=offset):
            pl.semaphore_signal(
                barrier, inc=1, device_id=place(*offset), device_id_type=pl.DeviceIdType.MESH
            )

    sends = ((0, 1), (0, -1), (1, 0), (1, 1), (1, -1))
    for slot, (seq_step, slab_step) in enumerate(sends):

        @pl.when(jnp.logical_not(present(-seq_step, -slab_step)))
        def _(slot=slot):
            if sends[slot][1]:
                halo_buf[slot] = jnp.zeros(halo_buf.shape[1:], BF16)
            else:
                center_buf[1] = jnp.zeros(center_buf.shape[1:], BF16)

    small[0].wait()
    scale = 1.0 + mod_buf[1:2, :]
    shift_high, shift_low = split_bf16(mod_buf[0:1, :])
    pick = lax.broadcasted_iota(jnp.int32, (EXTRA, width), 0)
    x_buf[tokens : tokens + EXTRA, :] = jnp.where(
        pick == 0,
        shift_high.astype(F32),
        jnp.where(pick == 1, shift_low.astype(F32), jnp.where(pick == 2, 1.0, 0.0)),
    ).astype(BF16)
    ones_row = lax.broadcasted_iota(jnp.int32, (EXTRA, width), 0) == 0
    rhs_buf[2 * patch : 2 * patch + EXTRA, :] = jnp.where(ones_row, 1.0, 0.0).astype(BF16)

    for copy in small[1:-1]:
        copy.wait()
    cell = order_buf[...].astype(F32) + 0.5
    per_frame = float(row_count * token_rows * token_cols)
    frame_all = jnp.floor(cell * (1.0 / per_frame))
    in_frame = cell - frame_all * per_frame
    frame_pos = frame_all - frames * jnp.floor((frame_all + 0.5) * (1.0 / frames))
    row_all = jnp.floor(in_frame * (1.0 / token_cols))
    column = in_frame - 0.5 - row_all * token_cols
    row_pos = row_all - token_rows * jnp.floor((row_all + 0.5) * (1.0 / token_rows))
    target = (frame_pos * token_rows + row_pos) * token_cols + column
    wanted = lax.broadcasted_iota(jnp.int32, (tokens, tokens), 0).astype(F32)
    one_hot = jnp.where(jnp.abs(wanted - target) < 0.25, 1.0, 0.0).astype(BF16)
    for f in range(frames):
        for a in range(2):
            for g in range(lines_buf.shape[2]):
                lines_buf[f, a, g : g + 1, :] = noisy_buf[f, a : a + 1, g * LANES : (g + 1) * LANES]
    lane = lax.broadcasted_iota(jnp.int32, (lines_buf.shape[2], LANES), 1)
    span = 2 * chan
    per_line = LANES // span
    groups = lines_buf.shape[2]
    for jj in range(per_line):
        line = jnp.zeros((groups, LANES), F32)
        for f in range(frames):
            for a in range(2):
                slot = f * 2 + a
                moved = lines_buf[f, a]
                if (slot - jj) % per_line:
                    moved = pltpu.roll(moved, ((slot - jj) * span) % LANES, 1)
                line = jnp.where((lane >= slot * span) & (lane < (slot + 1) * span), moved, line)
        latent_buf[pl.ds(jj, groups, stride=per_line), :] = line

    repeat = LANES // chan

    def lanes_of(ref):
        return jnp.concatenate([ref[...]] * repeat, axis=1)

    mean_row = lanes_of(mean_buf)
    std_row = lanes_of(std_buf)
    mix_row = lanes_of(mix_bias_buf)
    mix = jnp.concatenate([lanes_of(mix_buf)] * repeat, axis=0)
    mix_in = lax.broadcasted_iota(jnp.int32, (LANES, LANES), 0)
    mix_out = lax.broadcasted_iota(jnp.int32, (LANES, LANES), 1)
    group_in = lax.div(mix_in, chan)
    wanted_out = (
        lax.rem(lax.div(group_in, 2), 2) * (2 * frames)
        + lax.div(group_in, 4) * 2
        + lax.rem(group_in, 2)
    )
    same = wanted_out == lax.div(mix_out, chan)
    mix_high, mix_low = split_bf16(jnp.where(same, mix, 0.0))
    mix_both = jnp.concatenate([mix_high, mix_low], axis=1)

    at = index_ref[0]
    now = jnp.full((1, LANES), table_ref[at].astype(F32))
    later = jnp.full((1, LANES), table_ref[at + 1].astype(F32))
    step_size = later / 1000.0 - now / 1000.0

    weight_copy.wait()
    rhs_buf[0:patch, :] = (w_buf[...].astype(F32) * scale).astype(BF16)
    rhs_buf[patch : 2 * patch, :] = w_buf[...]

    block = 64
    blocks = tokens // block
    product = jnp.zeros((tokens + EXTRA, rhs_buf.shape[0]), F32)
    centers = [None] * blocks
    squares = [jnp.zeros((block, LANES), F32)] * blocks
    for part, hidden_copy in enumerate(loads):
        low = part * step
        hidden_copy.wait()
        product = product + dot_nt(x_buf[:, low : low + step], rhs_buf[:, low : low + step])
        for index in range(blocks):
            rows = slice(index * block, (index + 1) * block)
            if part == 0:
                total = x_buf[rows, 0:LANES].astype(F32)
                center = jnp.sum(total, axis=1, keepdims=True) * (1.0 / LANES)
                centers[index] = jnp.broadcast_to(center, (block, LANES))
            square = squares[index]
            for lane in range(low, low + step, LANES):
                gap = x_buf[rows, lane : lane + LANES].astype(F32) - centers[index]
                square = square + gap * gap
            squares[index] = square

    center = jnp.concatenate([value[:, 0:1] for value in centers], axis=0)
    spread = jnp.concatenate([jnp.sum(value, axis=1, keepdims=True) for value in squares], axis=0)
    average = product[0:tokens, 2 * patch : 2 * patch + 1] * (1.0 / width)
    spread = spread * (1.0 / width) - jnp.square(average - center)
    inverse = lax.rsqrt(spread + 1e-06)
    column_sum = product[tokens + 2 : tokens + 3, 0:patch]
    both = product[tokens : tokens + 1, :] + product[tokens + 1 : tokens + 2, :]
    offset_row = both[:, patch : 2 * patch]
    head = (product[0:tokens, 0:patch] - average * column_sum) * inverse + offset_row

    head_high, head_low = split_bf16(head)
    placed = dot_nn(one_hot, jnp.concatenate([head_high, head_low], axis=1))
    placed = placed[:, 0:patch] + placed[:, patch:]
    per = token_rows * token_cols
    for index in range(token_rows):
        pieces = [
            placed[f * per + index * token_cols : f * per + (index + 1) * token_cols, :]
            for f in range(frames)
        ]
        cells_buf[index] = jnp.concatenate(pieces, axis=1)

    slab_peers = (slab > 0).astype(jnp.int32) + (slab < slab_count - 1).astype(jnp.int32)
    seq_peers = (seq > 0).astype(jnp.int32) + (seq < seq_count - 1).astype(jnp.int32)
    pl.semaphore_wait(barrier, (1 + slab_peers) * (1 + seq_peers) - 1)

    pair = pltpu.make_async_remote_copy(
        src_ref=cells_buf.at[1 - half],
        dst_ref=partner_buf,
        send_sem=send_sem.at[0],
        recv_sem=recv_sem.at[0],
        device_id={"cfg": 1 - half},
        device_id_type=pl.DeviceIdType.MESH,
    )
    pair.start()

    pair.wait_recv()
    own = cells_buf[half]
    partner = partner_buf[...]
    cond = jnp.where(half == 0, own, partner)
    free = jnp.where(half == 0, partner, own)
    velocity = free + guidance_ref[0] * (cond - free)
    stepped = latent_buf[...] + step_size * velocity
    channels = stepped * std_row + mean_row
    high, low = split_bf16(channels)
    mixed = dot_nn(jnp.concatenate([high, low], axis=0), mix_both)
    mixed = mixed[0:token_cols, 0:LANES] + (
        mixed[0:token_cols, LANES:] + mixed[token_cols:, 0:LANES]
    )
    latent = (mixed + mix_row).astype(BF16)
    exact = latent.astype(F32)
    fold = token_cols // 2
    left = lax.broadcasted_iota(jnp.int32, (fold, LANES), 1) < LANES // 2
    first, second = exact[0:fold], exact[fold:]
    edge_buf[0] = jnp.where(left, first, pltpu.roll(second, LANES // 2, 1)).astype(BF16)
    edge_buf[1] = jnp.where(left, pltpu.roll(first, LANES // 2, 1), second).astype(BF16)
    center_buf[0] = latent

    copies = []
    for slot, (seq_step, slab_step) in enumerate(sends):
        if slab_step:
            source, target = edge_buf.at[(1 + slab_step) // 2], halo_buf.at[slot]
        else:
            source, target = center_buf.at[0], center_buf.at[1]
        copy = pltpu.make_async_remote_copy(
            src_ref=source,
            dst_ref=target,
            send_sem=send_sem.at[1 + slot],
            recv_sem=recv_sem.at[1 + slot],
            device_id=place(seq_step, slab_step),
            device_id_type=pl.DeviceIdType.MESH,
        )
        copies.append(copy)
    for slot in (3, 4, 2, 0, 1):
        pl.when(present(*sends[slot]))(copies[slot].start)

    small[-1].wait()
    position = 0
    for t in range(3):
        for shifted in range(2):
            for u in range(4):
                for e_in in range(2):
                    dx = (2 - 3 * e_in) if shifted else e_in
                    for e_out in range(2):
                        w = dx - e_out + 1
                        columns = slice(e_out * out_chan, (e_out + 1) * out_chan)
                        if u < 3 and 0 <= w <= 2:
                            value = conv_buf[(t * 3 + u) * 3 + w]
                        else:
                            value = jnp.zeros((chan, out_chan), BF16)
                        taps_buf[position : position + chan, columns] = value
                    position += chan

    lane = lax.broadcasted_iota(jnp.int32, (token_cols, LANES), 1)
    line = lax.broadcasted_iota(jnp.int32, (token_cols, LANES), 0)
    odd = lax.rem(lax.div(lane, chan), 2) == 1

    def turned(value, amount):
        return pltpu.roll(value, amount % LANES, 1) if amount % LANES else value

    def spread_rows(block, f, lane_base):
        return jnp.concatenate(
            [turned(block, lane_base - (part * frames + f) * span) for part in range(2)], axis=0
        )

    def middle_rows(block, f):
        return jnp.where(
            lane >= 2 * span, turned(block, -f * span), turned(block, span - f * span)
        )

    def tap_rows(full, above, below, f):
        full = jnp.where(lane < span, spread_rows(above, f, 0), full)
        full = jnp.where(lane >= 3 * span, spread_rows(below, f, 3 * span), full)
        before = jnp.where(line == 0, 0.0, pltpu.roll(full, 1, 0))
        after = jnp.where(line == token_cols - 1, 0.0, pltpu.roll(full, token_cols - 1, 0))
        beside = jnp.where(odd, before, after)
        upper = jnp.concatenate([full, beside], axis=1)
        lower = jnp.concatenate([turned(full, -span), turned(beside, -span)], axis=1)
        return jnp.concatenate([upper, lower], axis=0).astype(BF16)

    def arrived(slot):
        seq_step, slab_step = sends[slot]
        pl.when(present(-seq_step, -slab_step))(copies[slot].wait_recv)

    own_middle = [middle_rows(exact, f) for f in range(frames)]
    depth = 2 * LANES
    for slot in (2, 3, 4):
        arrived(slot)
    center_block = center_buf[1].astype(F32)
    above, below = halo_buf[3].astype(F32), halo_buf[4].astype(F32)
    earlier = [
        tap_rows(middle_rows(center_block, f), above, below, f) for f in range(frames)
    ]
    partial = []
    for f in range(frames):
        count = min(2, frames - f)
        partial.append(
            dot_nn(
                jnp.concatenate(earlier[f : f + count], axis=1), taps_buf[0 : count * depth, :]
            )
        )
    for slot in (0, 1):
        arrived(slot)
    above, below = halo_buf[0].astype(F32), halo_buf[1].astype(F32)
    current = [tap_rows(own_middle[f], above, below, f) for f in range(frames)]
    bias = conv_bias_buf[...]
    for f in range(frames):
        count = min(2, frames - f)
        result = partial[f] + dot_nn(
            jnp.concatenate(current[f + count - frames : f + 1], axis=1),
            taps_buf[count * depth :, :],
        )
        for y in range(2):
            first = (f * 2 + y) * token_cols
            for part in range(out_chan // LANES):
                lanes = slice(part * LANES, (part + 1) * LANES)
                for e in range(2):
                    from_lane = e * out_chan + part * LANES
                    wide_buf[part, pl.ds(2 * first + e, token_cols, stride=2), :] = (
                        result[y * token_cols : (y + 1) * token_cols, from_lane : from_lane + LANES]
                        + bias[part : part + 1, :]
                    )
                out_ref[f, y, :, lanes] = wide_buf[
                    part, 2 * first : 2 * first + 2 * token_cols, :
                ].astype(BF16)

    pair.wait_send()
    for slot in range(len(sends)):
        pl.when(present(*sends[slot]))(copies[slot].wait_send)


def per_device(
    counts,
    hidden,
    token_order,
    noisy_latent,
    head_weight,
    head_mod,
    guidance,
    timestep_index,
    step_table,
    vae_mean,
    vae_std,
    conv2_weight,
    conv2_bias,
    conv1_weight,
    conv1_bias,
):
    frames, lat_rows, lat_width = noisy_latent.shape
    chan = vae_mean.shape[0]
    tokens, width = hidden.shape[1:]
    patch = head_weight.shape[1]
    out_chan = conv1_weight.shape[2]
    token_cols = lat_width // (2 * chan)
    token_rows = lat_rows * counts[2] // 2
    chunks = 5
    operands = (
        hidden,
        token_order.reshape(1, -1),
        noisy_latent,
        head_weight.T,
        head_mod,
        guidance,
        timestep_index,
        step_table,
        vae_mean.reshape(1, -1),
        vae_std.reshape(1, -1),
        conv2_weight,
        conv2_bias.reshape(1, -1),
        conv1_weight,
        conv1_bias.reshape(-1, LANES),
    )
    block = (token_cols, LANES)
    scratch = [
        pltpu.VMEM((tokens + EXTRA, width), BF16),
        pltpu.VMEM((patch, width), BF16),
        pltpu.VMEM((2 * patch + EXTRA, width), BF16),
        pltpu.VMEM(operands[1].shape, jnp.int32),
        pltpu.VMEM(operands[2].shape, F32),
    ]
    scratch += [
        pltpu.VMEM(value.shape, value.dtype)
        for index, value in enumerate(operands)
        if index == 4 or index > 7
    ]
    scratch += [
        pltpu.VMEM((frames, lat_rows, lat_width // LANES, LANES), F32),
        pltpu.VMEM(block, F32),
        pltpu.VMEM((3 * 16 * chan, 2 * out_chan), BF16),
        pltpu.VMEM((token_rows,) + block, F32),
        pltpu.VMEM(block, F32),
        pltpu.VMEM((2,) + block, BF16),
        pltpu.VMEM((2, token_cols // 2, LANES), BF16),
        pltpu.VMEM((5, token_cols // 2, LANES), BF16),
        pltpu.VMEM((out_chan // LANES, frames * lat_rows * 2 * token_cols, LANES), F32),
        pltpu.SemaphoreType.DMA((9,)),
        pltpu.SemaphoreType.DMA((1 + chunks,)),
        pltpu.SemaphoreType.DMA((6,)),
        pltpu.SemaphoreType.DMA((6,)),
    ]
    sizes = tuple(counts) + (token_rows, token_cols, frames, chunks)
    return pl.pallas_call(
        functools.partial(kernel, sizes),
        out_shape=pltpu.VMEM((frames, lat_rows, 2 * token_cols, out_chan), BF16),
        in_specs=[
            pl.BlockSpec(memory_space=pltpu.SMEM if index in (5, 6, 7) else pl.ANY)
            for index in range(len(operands))
        ],
        out_specs=pl.BlockSpec(memory_space=pltpu.VMEM),
        scratch_shapes=scratch,
        compiler_params=pltpu.CompilerParams(
            collective_id=0, has_side_effects=True, vmem_limit_bytes=60 * 1024 * 1024
        ),
        name="guided_step",
    )(
        *[
            value
            if index in (5, 6, 7)
            else pltpu.with_memory_space_constraint(value, pltpu.HBM)
            for index, value in enumerate(operands)
        ]
    )


def solution(mesh):
    counts = (mesh.shape["seq"], mesh.shape["rows"], mesh.shape["cfg"])
    return jax.shard_map(
        functools.partial(per_device, counts),
        mesh=mesh,
        in_specs=(
            P("cfg", ("groups", "seq", "rows"), None),
            P(("groups", "seq", "rows")),
            P(("groups", "seq"), ("rows", "cfg"), None),
            P(),
            P(),
            P(),
            P(),
            P(),
            P(),
            P(),
            P(),
            P(),
            P(),
            P(),
        ),
        out_specs=P(("groups", "seq"), ("rows", "cfg"), None, None),
        check_vma=False,
    )
```
